128 devices in a mesh: lx: 8 (over z, core), ly: 8 (over y_hi, x), af: 2 (over y_lo).
Axes of the slice: x: 4, y: 4 (y_hi: 2, y_lo: 2; y = y_hi * 2 + y_lo), z: 4, core: 2. Of those that a mesh axis runs over, the one named last changes fastest.
Arguments:
- grad_out: bfloat16 [16, 64, 128, 320], P('af', 'lx', 'ly'), may hold values from -6 to 6
- inputs: bfloat16 [16, 64, 128, 320], P('af', 'lx', 'ly'), may hold values from -6 to 6
- weight: bfloat16 [27, 320, 320], P(None, 'af'), may hold values from -0.0625 to 0.0625
Outputs:
- grad_input: bfloat16 [16, 64, 128, 320], P('af', 'lx', 'ly')
- grad_weight: float32 [27, 320, 320], P(None, 'af', ('lx', 'ly'))
The draws below stay inside these ranges and needn't reach their ends.
All inputs are finite; a program needn't handle non-finite values.
Results may differ from the reference program's by a relative error of at most 0.01.
Values may be sent and summed in bfloat16 or wider, within the bound.
No kernel may reach another device: no remote copies, remote signals or barrier semaphores. Data moves between devices by JAX's collectives and lax.ppermute only.
A program may use at most 128 MiB of HBM per device.

```python
import math
import jax
import jax.numpy as jnp
from jax import lax

C = 320
DZ = 16
NX = 64
NY = 128


def shard_levels(stream_key, extent, cuts, low, high):
    gain, own = 1.0, jax.random.fold_in(stream_key, 6)
    for position, parts in cuts:
        heights = jnp.exp(jax.random.uniform(jax.random.fold_in(own, position), (parts,), jnp.float32, low / len(cuts), high / len(cuts)))
        gain = gain * jnp.repeat(heights, extent[position] // parts).reshape([-1 if axis == position else 1 for axis in range(len(extent))])
    return gain


def scatter_about(rng, dims, deviation, reach, shards=(), kind=jnp.bfloat16):
    drawn = jax.random.normal(rng, dims, jnp.float32) * deviation
    if len(shards) > 0:
        drawn = shard_levels(rng, dims, shards, -0.22, 0.18) * drawn
    return jnp.clip(drawn, min=-reach, max=reach).astype(kind)


def setup_inputs(seed: int = 0) -> dict:
    streams_of = jax.random.split(jax.random.key(seed), 4)
    return {
        "grad_out": scatter_about(streams_of[0], (DZ, NX, NY, C), 1.0, 6.0, ((0, 2), (1, 8), (2, 8))),
        "inputs": scatter_about(streams_of[1], (DZ, NX, NY, C), 1.0, 6.0, ((0, 2), (1, 8), (2, 8))),
        "weight": scatter_about(streams_of[2], (27, C, C), (27 * C) ** -0.5, 0.0625, ((1, 2),)),
    }


def offsets():
    return [(depth_off, row_off, col_off) for depth_off in range(3) for row_off in range(3) for col_off in range(3)]

def reference(grad_out, inputs, weight):
    depth, rows, cols, chans = inputs.shape
    cells = depth * rows * cols
    scale = 1.0 / math.sqrt(cells)
    widths = ((1, 1), (1, 1), (1, 1), (0, 0))
    padded_in = jnp.pad(inputs, widths)
    padded_grad = jnp.pad(grad_out, widths)
    flat_grad = grad_out.reshape(cells, chans)
    total = jnp.zeros((cells, chans), jnp.float32)
    pieces = []
    for index, (depth_off, row_off, col_off) in enumerate(offsets()):
        shifted = padded_in[depth_off:depth_off + depth, row_off:row_off + rows, col_off:col_off + cols, :].reshape(cells, chans)
        pieces.append(lax.dot_general(flat_grad, shifted, (((0,), (0,)), ((), ())), preferred_element_type=jnp.float32) * scale)
        moved = padded_grad[2 - depth_off:2 - depth_off + depth, 2 - row_off:2 - row_off + rows, 2 - col_off:2 - col_off + cols, :].reshape(cells, chans)
        total = total + jnp.dot(moved, weight[index], preferred_element_type=jnp.float32)
    grad_input = total.reshape(depth, rows, cols, chans).astype(jnp.bfloat16)
    return (grad_input, jnp.stack(pieces))
```

```python
import functools
import math

import jax
import jax.numpy as jnp
import numpy as np
from jax import lax
from jax.experimental import pallas as pl
from jax.experimental.pallas import tpu as pltpu
from jax.sharding import PartitionSpec as P

AXES = ("lx", "ly", "af")
BF, F32 = jnp.bfloat16, jnp.float32
C = 320
LIMIT = 56 * 2**20

STREAM_A = (0, 1, 2, 3, 4)
STREAM_B = (5, 6, 7, 8)


def routes(to):
    pairs = []
    for a in range(8):
        for b in range(8):
            for c in range(2):
                u, v, w = to(a, b, c)
                if 0 <= u < 8 and 0 <= v < 8:
                    pairs.append(((a * 8 + b) * 2 + c, (u * 8 + v) * 2 + w))
    return pairs


def send(value, to):
    return lax.ppermute(value, AXES, routes(to))


def swap_core(v):
    return send(v, lambda a, b, c: (a ^ 1, b, c))


def row_order():
    out = np.zeros((2, 4, 4, 2, 5, 2), np.int32)
    for first in range(4):
        for second in range(4):
            for d in range(2):
                for j in range(5):
                    out[0, first, second, d, j] = (first * 16 + d * 4 + second, j)
                    out[1, first, second, d, j] = (second * 16 + d * 4 + first, j)
    return out.reshape(320, 2)


def params():
    return pltpu.CompilerParams(vmem_limit_bytes=LIMIT)


def cost(flops, moved):
    return pl.CostEstimate(flops=flops, bytes_accessed=moved, transcendentals=0)


def sds(shape, dtype):
    return jax.ShapeDtypeStruct(shape, dtype)


def edges_kernel(g, first, last, plane, plane_first, plane_last):
    af = lax.axis_index("af")
    cells = g[...].reshape(1024, C)
    row = lax.broadcasted_iota(jnp.int32, (128, 1024), 0)
    col = lax.broadcasted_iota(jnp.int32, (128, 1024), 1)
    want = jnp.where(row < 64, row * 16, (row - 64) * 16 + 15)
    pick = jnp.where(col == want, 1.0, 0.0).astype(BF)
    both = jnp.dot(pick, cells, preferred_element_type=F32)
    low = both[:64].reshape(8, 8, C)
    high = both[64:].reshape(8, 8, C)
    first[...] = low.astype(BF)
    last[...] = high.astype(BF)
    at = (1 - af) * 7
    plane[...] = g[pl.ds(at, 1)].reshape(8, 16, C)
    plane_first[...] = jnp.where(af == 0, low[7], low[0]).astype(BF)
    plane_last[...] = jnp.where(af == 0, high[7], high[0]).astype(BF)


def edges(g):
    return pl.pallas_call(
        edges_kernel,
        out_shape=(
            sds((8, 8, C), BF),
            sds((8, 8, C), BF),
            sds((8, 16, C), BF),
            sds((8, C), BF),
            sds((8, C), BF),
        ),
        compiler_params=params(),
        cost_estimate=cost(100_000_000, 1_000_000),
        name="edges",
    )(g)


def rim_kernel(g, left, right, plane, plane_left, plane_right, halo, outer):
    core = lax.axis_index("lx") % 2
    lf, rf = left[...].astype(F32), right[...].astype(F32)
    pf, qf = plane_left[...].astype(F32), plane_right[...].astype(F32)
    for d in range(8):
        halo[d] = jnp.concatenate([lf[d], rf[d]], axis=0).astype(BF)
    halo[8:16] = plane[...]
    halo[16] = jnp.concatenate([pf, qf], axis=0).astype(BF)
    at = core * 7
    outer[0:8] = g[:, pl.ds(at, 1)].reshape(8, 16, C)
    outer[8] = plane[pl.ds(at, 1)].reshape(16, C)
    pad = jnp.zeros((7, C), F32)
    for n, (body, cap) in enumerate(((lf, pf), (rf, qf))):
        lo = jnp.concatenate([body[d, 0:1] for d in range(8)] + [cap[0:1], pad], axis=0)
        hi = jnp.concatenate([body[d, 7:8] for d in range(8)] + [cap[7:8], pad], axis=0)
        outer[9 + n] = jnp.where(core == 0, lo, hi).astype(BF)


def rim(g, left, right, plane, plane_left, plane_right):
    return pl.pallas_call(
        rim_kernel,
        out_shape=(sds((17, 16, C), BF), sds((11, 16, C), BF)),
        compiler_params=params(),
        cost_estimate=cost(1_000_000, 1_000_000),
        name="rim",
    )(g, left, right, plane, plane_left, plane_right)


def turn_kernel(order, own, other, out, both):
    core = lax.axis_index("lx") % 2
    mine = lax.axis_index("lx") * 8 + lax.axis_index("ly")
    both[:, pl.ds(core * 8, 8)] = own[...]
    both[:, pl.ds(8 - core * 8, 8)] = other[...]
    target = (order[:, 0:1] ^ mine) * 5 + order[:, 1:2]
    lane = lax.broadcasted_iota(jnp.int32, (320, C), 1)
    pick = jnp.where(lane == target, 1.0, 0.0).astype(BF)
    cells = both[...].reshape(2048, C)
    out[...] = lax.dot_general(
        pick, cells, (((1,), (1,)), ((), ())), preferred_element_type=F32
    ).astype(BF)


def turn(order, own, other):
    return pl.pallas_call(
        turn_kernel,
        out_shape=sds((320, 2048), BF),
        scratch_shapes=[pltpu.VMEM((8, 16, 16, C), BF)],
        compiler_params=params(),
        cost_estimate=cost(420_000_000, 2_600_000),
        name="turn",
    )(order, own, other)


def spread(tile, left, right):
    n = tile.shape[0]
    flat = tile.astype(F32).reshape(n * 16, C)
    col = lax.broadcasted_iota(jnp.int32, (n, 16, C), 1).reshape(n * 16, C)
    ends = jnp.broadcast_to(right.reshape(n, 1, C), (n, 16, C)).reshape(n * 16, C)
    heads = jnp.broadcast_to(left.reshape(n, 1, C), (n, 16, C)).reshape(n * 16, C)
    up = jnp.where(col == 15, ends, pltpu.roll(flat, n * 16 - 1, 0))
    down = jnp.where(col == 0, heads, pltpu.roll(flat, 1, 0))
    return jnp.concatenate([up, flat, down], axis=1).astype(BF).reshape(n, 16, 3 * C)


def weight_tiles(groups, turned, shifted, keep, sends):
    for n, pq in enumerate(groups):
        p, q = pq // 3, pq % 3
        cells = shifted[2 - p : 10 - p, 2 - q : 18 - q].reshape(2048, 3 * C)
        tile = jnp.dot(turned[...], cells, preferred_element_type=F32)
        keep[n] = tile[0:40]
        for b, ref in enumerate(sends):
            ref[n] = tile[40 * b + 40 : 40 * b + 80].astype(BF)


def first_kernel(g, other, halo, halo_other, alpha, beta, turned, kept_shifted, keep, s1, s2, s3, shifted, sem):
    core = lax.axis_index("lx") % 2
    af = lax.axis_index("af")
    for src, lines, at in ((g, halo, core * 8 + 1), (other, halo_other, 9 - core * 8)):

        def plane(d, carry, src=src, lines=lines, at=at):
            edge = lines[d].astype(F32)
            shifted[pl.ds(d + 1, 1), pl.ds(at, 8)] = spread(src[d], edge[0:8], edge[8:16])[None]
            return carry

        lax.fori_loop(0, 8, plane, 0)
        edge = lines[16].astype(F32)
        shifted[pl.ds(9 - af * 9, 1), pl.ds(at, 8)] = spread(lines[8:16], edge[0:8], edge[8:16])[None]
    for outer, at in ((alpha, core * 17), (beta, 17 - core * 17)):
        lf, rf = outer[9].astype(F32), outer[10].astype(F32)
        shifted[1:9, pl.ds(at, 1)] = spread(outer[0:8], lf[0:8], rf[0:8])[:, None]
        shifted[pl.ds(9 - af * 9, 1), pl.ds(at, 1)] = spread(outer[8:9], lf[8:9], rf[8:9])[None]
    shifted[pl.ds(af * 9, 1)] = jnp.zeros((1, 18, 16, 3 * C), BF)
    copy = pltpu.make_async_copy(shifted, kept_shifted, sem)
    copy.start()
    weight_tiles(STREAM_A, turned, shifted, keep, (s1, s2, s3))
    copy.wait()


def first_tiles(*operands):
    n = len(STREAM_A)
    piece = sds((n, 40, 3 * C), BF)
    spec = pl.BlockSpec(memory_space=pltpu.VMEM)
    return pl.pallas_call(
        first_kernel,
        out_shape=(sds((10, 18, 16, 3 * C), BF), sds((n, 40, 3 * C), F32), piece, piece, piece),
        in_specs=[spec] * 7,
        out_specs=(pl.BlockSpec(memory_space=pl.ANY),) + (spec,) * 4,
        scratch_shapes=[pltpu.VMEM((10, 18, 16, 3 * C), BF), pltpu.SemaphoreType.DMA],
        compiler_params=params(),
        cost_estimate=cost(2 * n * 160 * 2048 * 960, 14_000_000),
        name="first_tiles",
    )(*operands)


def second_kernel(shifted, turned, keep, s1, s2, s3):
    weight_tiles(STREAM_B, turned, shifted, keep, (s1, s2, s3))


def second_tiles(shifted, turned):
    n = len(STREAM_B)
    piece = sds((n, 40, 3 * C), BF)
    return pl.pallas_call(
        second_kernel,
        out_shape=(sds((n, 40, 3 * C), F32), piece, piece, piece),
        compiler_params=params(),
        cost_estimate=cost(2 * n * 160 * 2048 * 960, 10_000_000),
        name="second_tiles",
    )(shifted, turned)


def input_kernel(shifted_hbm, own_hbm, far_hbm, near_hbm, out, shifted, weight, sems):
    core = lax.axis_index("lx") % 2
    af = lax.axis_index("af")
    other = 160 - af * 160
    copies = [
        pltpu.make_async_copy(shifted_hbm.at[:, pl.ds(core * 8, 10)], shifted, sems.at[0]),
        pltpu.make_async_copy(own_hbm, weight.at[:, pl.ds(pl.multiple_of(af * 160, 16), 160)], sems.at[1]),
        pltpu.make_async_copy(far_hbm, weight.at[:, pl.ds(pl.multiple_of(other + core * 80, 16), 80)], sems.at[2]),
        pltpu.make_async_copy(
            near_hbm, weight.at[:, pl.ds(pl.multiple_of(other + 80 - core * 80, 16), 80)], sems.at[3]
        ),
    ]
    for copy in copies:
        copy.start()
    for copy in copies:
        copy.wait()

    def block(m, carry):
        total = jnp.zeros((256, C), F32)
        for p in range(3):
            for q in range(3):
                cells = shifted[pl.ds(2 * m + 2 - p, 2), 2 - q : 10 - q].reshape(256, 3 * C)
                taps = weight[9 * p + 3 * q : 9 * p + 3 * q + 3].reshape(3 * C, C)
                total = total + jnp.dot(cells, taps, preferred_element_type=F32)
        out[pl.ds(2 * m, 2)] = total.astype(BF).reshape(2, 8, 16, C)
        return carry

    lax.fori_loop(0, 4, block, 0)


def input_gradient(shifted, own, far, near):
    return pl.pallas_call(
        input_kernel,
        out_shape=sds((8, 8, 16, C), BF),
        in_specs=[pl.BlockSpec(memory_space=pl.ANY)] * 4,
        out_specs=pl.BlockSpec(memory_space=pltpu.VMEM),
        scratch_shapes=[
            pltpu.VMEM((10, 10, 16, 3 * C), BF),
            pltpu.VMEM((27, C, C), BF),
            pltpu.SemaphoreType.DMA((4,)),
        ],
        compiler_params=params(),
        cost_estimate=cost(2 * 1024 * 8640 * 320, 10_000_000),
        name="input_gradient",
    )(shifted, own, far, near)


def fold_kernel(n, keep, r1, r2, r3, out, s1, s2, s3):
    parts = [[], [], [], []]
    for g in range(n):
        total = keep[g] + r1[g].astype(F32) + r2[g].astype(F32) + r3[g].astype(F32)
        for b in range(4):
            parts[b].append(total[10 * b : 10 * b + 10])
    out[...] = jnp.concatenate(parts[0], axis=0)
    for b, ref in enumerate((s1, s2, s3)):
        ref[...] = jnp.concatenate(parts[b + 1], axis=0).astype(BF)


def fold(keep, r1, r2, r3):
    n = keep.shape[0]
    piece = sds((n * 10, 3 * C), BF)
    return pl.pallas_call(
        functools.partial(fold_kernel, n),
        out_shape=(sds((n * 10, 3 * C), F32), piece, piece, piece),
        compiler_params=params(),
        cost_estimate=cost(1_000_000, 2_500_000),
        name="fold",
    )(keep, r1, r2, r3)


def cut_kernel(a0, a1, a2, a3, b0, b1, b2, b3, out, s1, s2, s3):
    af = lax.axis_index("af")
    same, flip = [[], []], [[], []]
    for refs, n in (((a0, a1, a2, a3), len(STREAM_A)), ((b0, b1, b2, b3), len(STREAM_B))):
        total = refs[0][...]
        for ref in refs[1:]:
            total = total + ref[...].astype(F32)
        low = jnp.concatenate([total[:, C * r : C * r + 160] for r in range(3)], axis=1)
        high = jnp.concatenate([total[:, C * r + 160 : C * r + 320] for r in range(3)], axis=1)
        mine = jnp.where(af == 0, low, high)
        theirs = jnp.where(af == 0, high, low)
        for g in range(n):
            for d in range(2):
                same[d].append(mine[10 * g + 5 * d : 10 * g + 5 * d + 5])
                flip[d].append(theirs[10 * g + 5 * d : 10 * g + 5 * d + 5])
    out[...] = jnp.concatenate(same[0], axis=0)
    s1[...] = jnp.concatenate(flip[0], axis=0).astype(BF)
    s2[...] = jnp.concatenate(same[1], axis=0).astype(BF)
    s3[...] = jnp.concatenate(flip[1], axis=0).astype(BF)


def cut(*operands):
    piece = sds((45, 480), BF)
    return pl.pallas_call(
        cut_kernel,
        out_shape=(sds((45, 480), F32), piece, piece, piece),
        compiler_params=params(),
        cost_estimate=cost(1_000_000, 1_500_000),
        name="cut",
    )(*operands)


def last_kernel(scale, keep, r1, r2, r3, out):
    total = (keep[...] + r1[...].astype(F32) + r2[...].astype(F32) + r3[...].astype(F32)) * scale
    for n, pq in enumerate(STREAM_A + STREAM_B):
        for r in range(3):
            out[:, 3 * pq + r, :] = total[5 * n : 5 * n + 5, 160 * r : 160 * r + 160]


def last(scale, *operands):
    return pl.pallas_call(
        functools.partial(last_kernel, scale),
        out_shape=sds((5, 27, 160), F32),
        compiler_params=params(),
        cost_estimate=cost(100_000, 400_000),
        name="last",
    )(*operands)


def body(grad_out, inputs, weight):
    core = lax.axis_index("lx") % 2
    scale = 1.0 / math.sqrt(16 * 64 * 128)

    first, final, plane, plane_first, plane_final = edges(grad_out)
    left = send(final, lambda a, b, c: (a, b + 1, c))
    right = send(first, lambda a, b, c: (a, b - 1, c))
    plane = send(plane, lambda a, b, c: (a, b, c ^ 1))
    plane_left = send(plane_final, lambda a, b, c: (a, b + 1, c ^ 1))
    plane_right = send(plane_first, lambda a, b, c: (a, b - 1, c ^ 1))
    grad_other = swap_core(grad_out)
    inputs_other = swap_core(inputs)

    quarter = lax.dynamic_slice_in_dim(weight, core * 80, 80, 1)
    far = send(quarter, lambda a, b, c: (a, b ^ (4 * (a % 2)), c ^ 1))
    near = swap_core(far)

    halo, outer = rim(grad_out, left, right, plane, plane_left, plane_right)
    halo_other = swap_core(halo)
    alpha = send(outer, lambda a, b, c: (a + 2 * (a % 2) - 1, b, c))
    beta = send(outer, lambda a, b, c: (a + 4 * (a % 2) - 2, b, c))

    turned = turn(jnp.asarray(row_order()), inputs, inputs_other)
    shifted, a0, *a_out = first_tiles(
        grad_out, grad_other, halo, halo_other, alpha, beta, turned[:160]
    )
    along_z = [lambda a, b, c, s=s: (a ^ (2 * s), b, c) for s in (1, 2, 3)]
    along_x = [lambda a, b, c, s=s: (a, b ^ s, c) for s in (1, 2, 3)]
    along_y = [
        lambda a, b, c: (a, b, c ^ 1),
        lambda a, b, c: (a, b ^ 4, c),
        lambda a, b, c: (a, b ^ 4, c ^ 1),
    ]
    a_in = [send(v, to) for v, to in zip(a_out, along_z)]
    b0, *b_out = second_tiles(shifted, turned[160:])
    b_in = [send(v, to) for v, to in zip(b_out, along_x)]

    grad_input = input_gradient(shifted, weight, far, near)

    a0, *a_out = fold(a0, *a_in)
    a_in = [send(v, to) for v, to in zip(a_out, along_x)]
    b0, *b_out = fold(b0, *b_in)
    b_in = [send(v, to) for v, to in zip(b_out, along_z)]
    keep, *outs = cut(a0, *a_in, b0, *b_in)
    ins = [send(v, to) for v, to in zip(outs, along_y)]
    grad_weight = last(scale, keep, *ins)
    return (grad_input, jnp.transpose(grad_weight, (1, 2, 0)))


def solution(mesh):
    placed = (P("af", "lx", "ly", None), P("af", "lx", "ly", None), P(None, "af", None))
    return jax.shard_map(
        body,
        mesh=mesh,
        in_specs=placed,
        out_specs=(P("af", "lx", "ly", None), P(None, "af", ("lx", "ly"))),
        check_vma=False,
    )
```

```python
import functools
import math

import jax
import jax.numpy as jnp
import numpy as np
from jax import lax
from jax.experimental import pallas as pl
from jax.experimental.pallas import tpu as pltpu
from jax.sharding import PartitionSpec as P

AXES = ("lx", "ly", "af")
BF, F32 = jnp.bfloat16, jnp.float32
C = 320

STREAM_A = (0, 1, 2, 3, 4)
STREAM_B = (5, 6, 7, 8)


def routes(to):
    pairs = []
    for a in range(8):
        for b in range(8):
            for c in range(2):
                u, v, w = to(a, b, c)
                pairs.append(((a * 8 + b) * 2 + c, (u * 8 + v) * 2 + w))
    return pairs


def send(value, to):
    return lax.ppermute(value, AXES, routes(to))


def swap_core(v):
    return send(v, lambda a, b, c: (a ^ 1, b, c))


def row_order():
    out = np.zeros((2, 4, 4, 2, 5, 2), np.int32)
    steps = (0, 1, 3, 2)
    for m, first in enumerate(steps):
        for n, second in enumerate(steps):
            for d in range(2):
                for j in range(5):
                    out[0, m, n, d, j] = (first * 16 + d * 4 + second, j)
                    out[1, m, n, d, j] = (second * 16 + d * 4 + first, j)
    return out.reshape(320, 2)


def params(mib=8):
    return pltpu.CompilerParams(vmem_limit_bytes=mib * 2**20)


BRIEF = pl.CostEstimate(flops=1, bytes_accessed=1, transcendentals=0)


def sds(shape, dtype):
    return jax.ShapeDtypeStruct(shape, dtype)


def edges_kernel(g, other, alpha, beta, line, half, corner, outer, plane):
    core = lax.axis_index("lx") % 2
    at = 7 - lax.axis_index("af") * 7
    column = jnp.where(lax.axis_index("ly") % 2 == core, 15, 0)

    def picker(rows, tiles):
        row = lax.broadcasted_iota(jnp.int32, (rows, 16 * tiles), 0)
        cell = lax.broadcasted_iota(jnp.int32, (rows, 16 * tiles), 1)
        return jnp.where(cell == row * 16 + column, 1.0, 0.0).astype(BF)

    pick = picker(8, 8)

    def ends(tile, to):
        got = jnp.dot(pick, tile.reshape(128, C), preferred_element_type=F32)
        line[pl.ds(to, 1)] = got.astype(BF)[None]

    for src, to in ((g, core * 8 + 1), (other, 9 - core * 8)):
        for n in range(8):
            ends(src[:, n], to + n)
        plane[pl.ds(to, 8)] = src[pl.ds(at, 1)].reshape(8, 16, C)
    z = lax.axis_index("lx") // 2
    for n, src in enumerate((alpha, beta)):
        to = 17 * (core ^ n)
        inside = jnp.where(to == 0, z > 0, z < 3)
        outer[n] = jnp.where(inside, src[...].astype(F32), 0.0).astype(BF)
        ends(outer[n], to)
        plane[pl.ds(to, 1)] = outer[n, pl.ds(at, 1)]
    half[...] = plane[pl.ds(9 * core, 9)]
    got = jnp.dot(picker(24, 18), plane[...].reshape(288, C), preferred_element_type=F32)
    corner[...] = got[:18].astype(BF)


def edges(g, other, alpha, beta):
    return pl.pallas_call(
        edges_kernel,
        out_shape=(
            sds((18, 8, C), BF),
            sds((9, 16, C), BF),
            sds((18, C), BF),
            sds((2, 8, 16, C), BF),
        ),
        scratch_shapes=[pltpu.VMEM((18, 16, C), BF)],
        compiler_params=params(10),
        cost_estimate=BRIEF,
        name="edges",
    )(g, other, alpha, beta)


def turn_kernel(order, own, other, out_a, out_b, both):
    core = lax.axis_index("lx") % 2
    mine = lax.axis_index("lx") * 8 + lax.axis_index("ly")
    both[:, pl.ds(core * 8, 8)] = own[...]
    both[:, pl.ds(8 - core * 8, 8)] = other[...]
    target = (order[:, 0:1] ^ mine) * 5 + order[:, 1:2]
    lane = lax.broadcasted_iota(jnp.int32, (320, C), 1)
    pick = jnp.where(lane == target, 1.0, 0.0).astype(BF)
    cells = both[...].reshape(2048, C)
    out = lax.dot_general(
        pick, cells, (((1,), (1,)), ((), ())), preferred_element_type=F32
    ).astype(BF)
    out_a[...] = out[:160]
    out_b[...] = out[160:]


def turn(order, own, other):
    return pl.pallas_call(
        turn_kernel,
        out_shape=(sds((160, 2048), BF), sds((160, 2048), BF)),
        scratch_shapes=[pltpu.VMEM((8, 16, 16, C), BF)],
        compiler_params=params(12),
        cost_estimate=BRIEF,
        name="turn",
    )(order, own, other)


def spread(tile, left, right):
    n = tile.shape[0]
    flat = tile.astype(F32).reshape(n * 16, C)
    col = lax.broadcasted_iota(jnp.int32, (n, 16, C), 1).reshape(n * 16, C)
    ends = jnp.broadcast_to(right.reshape(n, 1, C), (n, 16, C)).reshape(n * 16, C)
    heads = jnp.broadcast_to(left.reshape(n, 1, C), (n, 16, C)).reshape(n * 16, C)
    up = jnp.where(col == 15, ends, pltpu.roll(flat, n * 16 - 1, 0))
    down = jnp.where(col == 0, heads, pltpu.roll(flat, 1, 0))
    return jnp.concatenate([up, flat, down], axis=1).astype(BF).reshape(n, 16, 3 * C)


def weight_tiles(groups, turned, shifted, keep, sends):
    for n, pq in enumerate(groups):
        p, q = pq // 3, pq % 3
        cells = shifted[2 - p : 10 - p, 2 - q : 18 - q].reshape(2048, 3 * C)
        tile = jnp.dot(turned[...], cells, preferred_element_type=F32)
        keep[n] = tile[0:40]
        for b, ref in enumerate(sends):
            ref[n] = tile[40 * b + 40 : 40 * b + 80].astype(BF)


def first_kernel(
    g, other, outer, line, line_other, half, half_other, corner, corner_other, turned,
    kept_shifted, keep, s1, s2, s3, shifted, plane, sem,
):
    core = lax.axis_index("lx") % 2
    af = lax.axis_index("af")

    ly = lax.axis_index("ly")
    side = ly % 2

    def order(mine, theirs):
        mine, theirs = mine.astype(F32), theirs.astype(F32)
        left = jnp.where(side == core, theirs, mine)
        right = jnp.where(side == core, mine, theirs)
        return jnp.where(ly > 0, left, 0.0), jnp.where(ly < 7, right, 0.0)

    def put(tile, at):
        lines = order(line[pl.ds(at, 1)][0], line_other[pl.ds(at, 1)][0])
        shifted[1:9, pl.ds(at, 1)] = spread(tile, *lines)[:, None]

    for src, at in ((g, core * 8 + 1), (other, 9 - core * 8)):

        def row(n, carry, src=src, at=at):
            put(src[:, pl.ds(n, 1)].reshape(8, 16, C), at + n)
            return carry

        lax.fori_loop(0, 8, row, 0)
    put(outer[0], core * 17)
    put(outer[1], 17 - core * 17)
    plane[pl.ds(9 * core, 9)] = half[...]
    plane[pl.ds(9 - 9 * core, 9)] = half_other[...]
    lines = order(corner[...], corner_other[...])
    shifted[pl.ds(9 - af * 9, 1)] = spread(plane[...], *lines)[None]
    shifted[pl.ds(af * 9, 1)] = jnp.zeros((1, 18, 16, 3 * C), BF)
    copy = pltpu.make_async_copy(shifted, kept_shifted, sem)
    copy.start()
    weight_tiles(STREAM_A, turned, shifted, keep, (s1, s2, s3))
    copy.wait()


def first_tiles(*operands):
    n = len(STREAM_A)
    piece = sds((n, 40, 3 * C), BF)
    spec = pl.BlockSpec(memory_space=pltpu.VMEM)
    return pl.pallas_call(
        first_kernel,
        out_shape=(sds((10, 18, 16, 3 * C), BF), sds((n, 40, 3 * C), F32), piece, piece, piece),
        in_specs=[spec] * 10,
        out_specs=(pl.BlockSpec(memory_space=pl.ANY),) + (spec,) * 4,
        scratch_shapes=[
            pltpu.VMEM((10, 18, 16, 3 * C), BF),
            pltpu.VMEM((18, 16, C), BF),
            pltpu.SemaphoreType.DMA,
        ],
        compiler_params=params(24),
        cost_estimate=BRIEF,
        name="first_tiles",
    )(*operands)


def second_kernel(shifted, turned, keep, s1, s2, s3):
    weight_tiles(STREAM_B, turned, shifted, keep, (s1, s2, s3))


def second_tiles(shifted, turned):
    n = len(STREAM_B)
    piece = sds((n, 40, 3 * C), BF)
    return pl.pallas_call(
        second_kernel,
        out_shape=(sds((n, 40, 3 * C), F32), piece, piece, piece),
        compiler_params=params(16),
        cost_estimate=BRIEF,
        name="second_tiles",
    )(shifted, turned)


def input_kernel(start, planes, *refs):
    shifted_hbm, own_hbm, far_hbm, near_hbm = refs[:4]
    out, shifted, weight, total, done, sems = refs[-6:]
    core = lax.axis_index("lx") % 2
    af = lax.axis_index("af")
    other = 160 - af * 160
    rows = pl.ds(core * 8, 10)
    pieces = (
        (own_hbm, 160, af * 160),
        (far_hbm, 80, other + core * 80),
        (near_hbm, 80, other + 80 - core * 80),
    )
    copies = []
    for n, p in enumerate((2, 1, 0)):
        low, high = (0, planes) if n == 0 else (planes + n - 1, planes + n)
        some = [
            pltpu.make_async_copy(
                shifted_hbm.at[start + low : start + high, rows], shifted.at[low:high], sems.at[4 * n]
            )
        ]
        for m, (src, size, to) in enumerate(pieces):
            some.append(
                pltpu.make_async_copy(
                    src.at[9 * p : 9 * p + 9],
                    weight.at[9 * p : 9 * p + 9, pl.ds(pl.multiple_of(to, 16), size)],
                    sems.at[4 * n + 1 + m],
                )
            )
        for copy in some:
            copy.start()
        copies.append(some)
    for n, p in enumerate((2, 1, 0)):
        for copy in copies[n]:
            copy.wait()

        def block(m, carry, n=n, p=p):
            value = jnp.zeros((256, C), F32)
            for q in range(3):
                cells = shifted[pl.ds(2 * m + 2 - p, 2), 2 - q : 10 - q].reshape(256, 3 * C)
                taps = weight[9 * p + 3 * q : 9 * p + 3 * q + 3].reshape(3 * C, C)
                value = value + jnp.dot(cells, taps, preferred_element_type=F32)
            if n > 0:
                value = value + total[m]
            if n < 2:
                total[m] = value
            else:
                done[pl.ds(2 * m, 2)] = value.astype(BF).reshape(2, 8, 16, C)
            return carry

        lax.fori_loop(0, planes // 2, block, 0)
    copy = pltpu.make_async_copy(done, out.at[start : start + planes], sems.at[12])
    copy.start()
    copy.wait()


def input_gradient(start, planes, operands, so_far=None):
    operands = list(operands) + ([] if so_far is None else [so_far])
    spec = pl.BlockSpec(memory_space=pl.ANY)
    return pl.pallas_call(
        functools.partial(input_kernel, start, planes),
        out_shape=sds((8, 8, 16, C), BF),
        in_specs=[spec] * len(operands),
        out_specs=spec,
        input_output_aliases={} if so_far is None else {4: 0},
        scratch_shapes=[
            pltpu.VMEM((planes + 2, 10, 16, 3 * C), BF),
            pltpu.VMEM((27, C, C), BF),
            pltpu.VMEM((planes // 2, 256, C), F32),
            pltpu.VMEM((planes, 8, 16, C), BF),
            pltpu.SemaphoreType.DMA((13,)),
        ],
        compiler_params=params(18),
        cost_estimate=BRIEF,
        name="input_gradient",
    )(*operands)


def quarters(blocks):
    return [jnp.concatenate([v[10 * b : 10 * b + 10] for v in blocks], axis=0) for b in range(4)]


def fold_kernel(n, keep, r1, r2, r3, out, s1, s2, s3):
    blocks = [keep[g] + r1[g].astype(F32) + r2[g].astype(F32) + r3[g].astype(F32) for g in range(n)]
    parts = quarters(blocks)
    out[...] = parts[0]
    for b, ref in enumerate((s1, s2, s3)):
        ref[...] = parts[b + 1].astype(BF)


def fold(keep, ins):
    n = keep.shape[0]
    piece = sds((n * 10, 3 * C), BF)
    return pl.pallas_call(
        functools.partial(fold_kernel, n),
        out_shape=(sds((n * 10, 3 * C), F32), piece, piece, piece),
        compiler_params=params(),
        cost_estimate=BRIEF,
        name="fold",
    )(keep, *ins)


def cut_kernel(a0, a1, a2, a3, b0, b1, b2, b3, out, s1, s2, s3):
    af = lax.axis_index("af")
    same, flip = [[], []], [[], []]
    for refs, n in (((a0, a1, a2, a3), len(STREAM_A)), ((b0, b1, b2, b3), len(STREAM_B))):
        total = refs[0][...]
        for ref in refs[1:]:
            total = total + ref[...].astype(F32)
        low = jnp.concatenate([total[:, C * r : C * r + 160] for r in range(3)], axis=1)
        high = jnp.concatenate([total[:, C * r + 160 : C * r + 320] for r in range(3)], axis=1)
        mine = jnp.where(af == 0, low, high)
        theirs = jnp.where(af == 0, high, low)
        for g in range(n):
            for d in range(2):
                same[d].append(mine[10 * g + 5 * d : 10 * g + 5 * d + 5])
                flip[d].append(theirs[10 * g + 5 * d : 10 * g + 5 * d + 5])
    out[...] = jnp.concatenate(same[0], axis=0)
    s1[...] = jnp.concatenate(flip[0], axis=0).astype(BF)
    s2[...] = jnp.concatenate(same[1], axis=0).astype(BF)
    s3[...] = jnp.concatenate(flip[1], axis=0).astype(BF)


def cut(*operands):
    piece = sds((45, 480), BF)
    return pl.pallas_call(
        cut_kernel,
        out_shape=(sds((45, 480), F32), piece, piece, piece),
        compiler_params=params(),
        cost_estimate=BRIEF,
        name="cut",
    )(*operands)


def last_kernel(scale, keep, r1, r2, r3, out):
    total = (keep[...] + r1[...].astype(F32) + r2[...].astype(F32) + r3[...].astype(F32)) * scale
    for n, pq in enumerate(STREAM_A + STREAM_B):
        for r in range(3):
            out[:, 3 * pq + r, :] = total[5 * n : 5 * n + 5, 160 * r : 160 * r + 160]


def last(scale, *operands):
    return pl.pallas_call(
        functools.partial(last_kernel, scale),
        out_shape=sds((5, 27, 160), F32),
        compiler_params=params(),
        cost_estimate=BRIEF,
        name="last",
    )(*operands)


def body(grad_out, inputs, weight):
    core = lax.axis_index("lx") % 2
    scale = 1.0 / math.sqrt(16 * 64 * 128)

    grad_other = swap_core(grad_out)
    inputs_other = swap_core(inputs)
    outer = lax.dynamic_slice_in_dim(grad_out, core * 7, 1, 1).reshape(8, 16, C)
    weight_late, outer = lax.optimization_barrier((weight, outer))
    quarter = lax.dynamic_slice_in_dim(weight_late, core * 80, 80, 1)
    alpha = send(outer, lambda a, b, c: ((a + 2 * (a % 2) - 1) % 8, b, c))
    alpha, grad_other, inputs_other, _ = lax.optimization_barrier(
        (alpha, grad_other, inputs_other, quarter)
    )
    beta = swap_core(alpha)

    line, plane, corner, outer = edges(grad_out, grad_other, alpha, beta)

    def side(a, b):
        return b ^ 1 if a % 2 == 0 else (b + 2 * (b % 2) - 1) % 8

    line = send(line, lambda a, b, c: (a, side(a, b), c))
    corner = send(corner, lambda a, b, c: (a, side(a, b), c ^ 1))
    plane = send(plane, lambda a, b, c: (a, b, c ^ 1))
    turned_a, turned_b = turn(jnp.asarray(row_order()), inputs, inputs_other)
    line, corner, plane, turned_a = lax.optimization_barrier((line, corner, plane, turned_a))
    line_other, corner_other, plane_other = swap_core(line), swap_core(corner), swap_core(plane)

    quarter, line = lax.optimization_barrier((quarter, line))
    far = send(quarter, lambda a, b, c: (a, b ^ (4 * (a % 2)), c ^ 1))

    shifted, a0, *a_out = first_tiles(
        grad_out, grad_other, outer,
        line, line_other, plane, plane_other, corner, corner_other, turned_a,
    )
    along_z = [lambda a, b, c, s=s: (a ^ (2 * s), b, c) for s in (1, 3, 2)]
    along_x = [lambda a, b, c, s=s: (a, b ^ s, c) for s in (1, 3, 2)]
    along_y = [
        lambda a, b, c: (a, b, c ^ 1),
        lambda a, b, c: (a, b ^ 4, c),
        lambda a, b, c: (a, b ^ 4, c ^ 1),
    ]
    a_in = [send(v, to) for v, to in zip(a_out[:2], along_z)]
    b0, *b_out = second_tiles(shifted, turned_b)
    b_in = [send(v, to) for v, to in zip(b_out[:2], along_x)]
    a_late, b_late = a_out[2], b_out[2]
    far, b0, a_in[0], a_in[1], a_late, b_late = lax.optimization_barrier(
        (far, b0, a_in[0], a_in[1], a_late, b_late)
    )
    near = swap_core(far)
    a_in.append(send(a_late, along_z[2]))
    b_in.append(send(b_late, along_x[2]))

    operands = (shifted, weight, far, near)
    grad_input = input_gradient(0, 6, operands)
    grad_input, *a_in = lax.optimization_barrier((grad_input, *a_in))
    a0, *a_out = fold(a0, a_in)
    a0, *b_in = lax.optimization_barrier((a0, *b_in))
    a_in = [send(v, to) for v, to in zip(a_out, along_x)]
    b0, *b_out = fold(b0, b_in)
    b_in = [send(v, to) for v, to in zip(b_out, along_z)]
    grad_input, b0 = lax.optimization_barrier((grad_input, b0))
    grad_input = input_gradient(6, 2, operands, grad_input)
    grad_input, *b_in = lax.optimization_barrier((grad_input, *b_in))
    keep, *outs = cut(a0, *a_in, b0, *b_in)
    ins = [send(v, to) for v, to in zip(outs, along_y)]
    grad_weight = last(scale, keep, *ins)
    return (grad_input, jnp.transpose(grad_weight, (1, 2, 0)))


def solution(mesh):
    placed = (P("af", "lx", "ly", None), P("af", "lx", "ly", None), P(None, "af", None))
    return jax.shard_map(
        body,
        mesh=mesh,
        in_specs=placed,
        out_specs=(P("af", "lx", "ly", None), P(None, "af", ("lx", "ly"))),
        check_vma=False,
    )
```

```python
import functools
import math

import jax
import jax.numpy as jnp
from jax import lax
from jax.experimental import pallas as pl
from jax.experimental.pallas import tpu as pltpu
from jax.sharding import PartitionSpec as P

AXES = ("lx", "ly", "af")
BF, F32 = jnp.bfloat16, jnp.float32
C = 320
HALF = 512
LANES = 2 * HALF

STREAM_A = (0, 1, 2, 3, 4)
STREAM_B = (5, 6, 7, 8)


def routes(to):
    pairs = []
    for a in range(8):
        for b in range(8):
            for c in range(2):
                u, v, w = to(a, b, c)
                pairs.append(((a * 8 + b) * 2 + c, (u * 8 + v) * 2 + w))
    return pairs


def send(value, to):
    return lax.ppermute(value, AXES, routes(to))


def swap_core(v):
    return send(v, lambda a, b, c: (a ^ 1, b, c))


def params(mib=8):
    return pltpu.CompilerParams(vmem_limit_bytes=mib * 2**20)


BRIEF = pl.CostEstimate(flops=1, bytes_accessed=1, transcendentals=0)


def sds(shape, dtype):
    return jax.ShapeDtypeStruct(shape, dtype)


def edges_kernel(g, other, alpha, beta, line, half, corner, outer, plane):
    core = lax.axis_index("lx") % 2
    at = 7 - lax.axis_index("af") * 7
    column = jnp.where(lax.axis_index("ly") % 2 == core, 15, 0)

    def picker(rows, tiles):
        row = lax.broadcasted_iota(jnp.int32, (rows, 16 * tiles), 0)
        cell = lax.broadcasted_iota(jnp.int32, (rows, 16 * tiles), 1)
        return jnp.where(cell == row * 16 + column, 1.0, 0.0).astype(BF)

    pick = picker(8, 8)

    def ends(tile, to):
        got = jnp.dot(pick, tile.reshape(128, C), preferred_element_type=F32)
        line[pl.ds(to, 1)] = got.astype(BF)[None]

    for src, to in ((g, core * 8 + 1), (other, 9 - core * 8)):
        for n in range(8):
            ends(src[:, n], to + n)
        plane[pl.ds(to, 8)] = src[pl.ds(at, 1)].reshape(8, 16, C)
    z = lax.axis_index("lx") // 2
    for n, src in enumerate((alpha, beta)):
        to = 17 * (core ^ n)
        inside = jnp.where(to == 0, z > 0, z < 3)
        outer[n] = jnp.where(inside, src[...].astype(F32), 0.0).astype(BF)
        ends(outer[n], to)
        plane[pl.ds(to, 1)] = outer[n, pl.ds(at, 1)]
    half[...] = plane[pl.ds(9 * core, 9)]
    got = jnp.dot(picker(24, 18), plane[...].reshape(288, C), preferred_element_type=F32)
    corner[...] = got[:18].astype(BF)


def edges(g, other, alpha, beta):
    return pl.pallas_call(
        edges_kernel,
        out_shape=(
            sds((18, 8, C), BF),
            sds((9, 16, C), BF),
            sds((18, C), BF),
            sds((2, 8, 16, C), BF),
        ),
        scratch_shapes=[pltpu.VMEM((18, 16, C), BF)],
        compiler_params=params(10),
        cost_estimate=BRIEF,
        name="edges",
    )(g, other, alpha, beta)


def turn_kernel(own, other, out_a, out_b, both):
    core = lax.axis_index("lx") % 2
    mine = lax.axis_index("lx") * 8 + lax.axis_index("ly")
    both[:, pl.ds(core * 8, 8)] = own[...]
    both[:, pl.ds(8 - core * 8, 8)] = other[...]
    cells = both[...].reshape(2048, C)
    row = lax.broadcasted_iota(jnp.int32, (160, C), 0)
    fives, tens, forties = row * 13108 >> 16, row * 6554 >> 16, row * 52429 >> 21
    first, second = forties, tens & 3
    first, second = first ^ (first >> 1), second ^ (second >> 1)
    lane = lax.broadcasted_iota(jnp.int32, (160, C), 1)
    for out, z, x in ((out_a, first, second), (out_b, second, first)):
        chunk = mine ^ (z * 16 + (fives & 1) * 4 + x)
        target = chunk * 5 + row - fives * 5
        pick = jnp.where(lane == target, 1.0, 0.0).astype(BF)
        out[...] = lax.dot_general(
            pick, cells, (((1,), (1,)), ((), ())), preferred_element_type=F32
        ).astype(BF)


def turn(own, other):
    return pl.pallas_call(
        turn_kernel,
        out_shape=(sds((160, 2048), BF), sds((160, 2048), BF)),
        scratch_shapes=[pltpu.VMEM((8, 16, 16, C), BF)],
        compiler_params=params(12),
        cost_estimate=BRIEF,
        name="turn",
    )(own, other)


def spread(tile, left, right):
    n = tile.shape[0]
    rows = n * 16
    flat = tile.astype(F32).reshape(rows, C)
    col = lax.broadcasted_iota(jnp.int32, (n, 16, C), 1).reshape(rows, C)
    ends = jnp.broadcast_to(right.reshape(n, 1, C), (n, 16, C)).reshape(rows, C)
    heads = jnp.broadcast_to(left.reshape(n, 1, C), (n, 16, C)).reshape(rows, C)
    up = jnp.where(col == 15, ends, pltpu.roll(flat, rows - 1, 0)).astype(BF)
    down = jnp.where(col == 0, heads, pltpu.roll(flat, 1, 0)).astype(BF)
    shifts = (up, tile.reshape(rows, C), down)
    pad = jnp.zeros((rows, HALF - 480), BF)
    lanes = [v[:, :160] for v in shifts] + [pad] + [v[:, 160:] for v in shifts] + [pad]
    return jnp.concatenate(lanes, axis=1).reshape(n, 16, LANES)


def tiles_kernel(
    g, other, outer, line, line_other, half, half_other, corner, corner_other, turned_a, turned_b,
    shifted, keep_a, a1, a3, a_low, a_high, keep_b, b1, b3, b_low, b_high, plane,
):
    core = lax.axis_index("lx") % 2
    af = lax.axis_index("af")
    ly = lax.axis_index("ly")
    side = ly % 2

    def order(mine, theirs):
        mine, theirs = mine.astype(F32), theirs.astype(F32)
        left = jnp.where(side == core, theirs, mine)
        right = jnp.where(side == core, mine, theirs)
        return jnp.where(ly > 0, left, 0.0), jnp.where(ly < 7, right, 0.0)

    def put(tile, at):
        lines = order(line[pl.ds(at, 1)][0], line_other[pl.ds(at, 1)][0])
        shifted[1:9, pl.ds(at, 1)] = spread(tile, *lines)[:, None]

    for src, at in ((g, core * 8 + 1), (other, 9 - core * 8)):

        def row(n, carry, src=src, at=at):
            put(src[:, pl.ds(n, 1)].reshape(8, 16, C), at + n)
            return carry

        lax.fori_loop(0, 8, row, 0, unroll=4)
    put(outer[0], core * 17)
    put(outer[1], 17 - core * 17)
    plane[pl.ds(9 * core, 9)] = half[...]
    plane[pl.ds(9 - 9 * core, 9)] = half_other[...]
    lines = order(corner[...], corner_other[...])
    shifted[pl.ds(9 - af * 9, 1)] = spread(plane[...], *lines)[None]
    shifted[pl.ds(af * 9, 1)] = jnp.zeros((1, 18, 16, LANES), BF)
    for groups, turned, keep, near, low, high in (
        (STREAM_A, turned_a, keep_a, (a1, a3), a_low, a_high),
        (STREAM_B, turned_b, keep_b, (b1, b3), b_low, b_high),
    ):
        for n, pq in enumerate(groups):
            p, q = pq // 3, pq % 3
            cells = shifted[2 - p : 10 - p, 2 - q : 18 - q].reshape(2048, LANES)
            tile = jnp.dot(turned[...], cells, preferred_element_type=F32)
            keep[n] = tile[0:40]
            for b, ref in enumerate(near):
                ref[n] = tile[40 * b + 40 : 40 * b + 80]
            low[n] = tile[120:160, :HALF].astype(BF)
            high[n] = tile[120:160, HALF:].astype(BF)


def tiles(*operands):
    outs = [sds((10, 18, 16, LANES), BF)]
    for stream in (STREAM_A, STREAM_B):
        n = len(stream)
        outs += [sds((n, 40, LANES), F32)] * 3 + [sds((n, 40, HALF), BF)] * 2
    return pl.pallas_call(
        tiles_kernel,
        out_shape=tuple(outs),
        scratch_shapes=[pltpu.VMEM((18, 16, C), BF)],
        compiler_params=params(28),
        cost_estimate=BRIEF,
        name="tiles",
    )(*operands)


def join_kernel(a1, a3, a_low, a_high, b1, b3, b_low, b_high, a1_out, a3_out, b1_out, b3_out):
    for one, three, low, high, one_out, three_out in (
        (a1, a3, a_low, a_high, a1_out, a3_out),
        (b1, b3, b_low, b_high, b1_out, b3_out),
    ):
        one_out[:, :, :HALF] = one[:, :, :HALF].astype(BF)
        one_out[:, :, HALF:] = (one[:, :, HALF:] + high[...].astype(F32)).astype(BF)
        three_out[:, :, :HALF] = (three[:, :, :HALF] + low[...].astype(F32)).astype(BF)
        three_out[:, :, HALF:] = three[:, :, HALF:].astype(BF)


def join(a1, a3, a_low, a_high, b1, b3, b_low, b_high):
    outs = [sds(v.shape, BF) for v in (a1, a3, b1, b3)]
    return pl.pallas_call(
        join_kernel,
        out_shape=tuple(outs),
        compiler_params=params(12),
        cost_estimate=BRIEF,
        name="join",
    )(a1, a3, a_low, a_high, b1, b3, b_low, b_high)


def flipped(weight, pq, start, rows):
    row = lax.broadcasted_iota(jnp.int32, (rows, C), 0)
    lane = lax.broadcasted_iota(jnp.int32, (rows, C), 1)
    pick = jnp.where(lane == row + start, 1.0, 0.0).astype(BF)
    taps = weight[3 * pq : 3 * pq + 3].reshape(480, C)
    turned = lax.dot_general(pick, taps, (((1,), (1,)), ((), ())), preferred_element_type=F32)
    return jnp.concatenate([turned.astype(BF), jnp.zeros((rows, HALF - 480), BF)], axis=1)


def flip_kernel(weight, out):
    core = lax.axis_index("lx") % 2
    for pq in range(9):
        out[pq] = flipped(weight, pq, core * 160, 160)


def flip(weight):
    return pl.pallas_call(
        flip_kernel,
        out_shape=sds((9, 160, HALF), BF),
        compiler_params=params(20),
        cost_estimate=BRIEF,
        name="flip",
    )(weight)


def half_sum(shifted, taps, first, emit):
    core = lax.axis_index("lx") % 2
    lanes = pl.ds(pl.multiple_of(first * HALF, HALF), HALF)
    for p in range(3):
        value = None
        for q in range(3):
            rows = pl.ds(core * 8 + 2 - q, 8)
            cells = shifted[2 - p : 10 - p, rows, :, lanes].reshape(1024, HALF)
            term = lax.dot_general(
                taps(3 * p + q), cells, (((1,), (1,)), ((), ())), preferred_element_type=F32
            )
            value = term if value is None else value + term
        emit(p, value)


def own_kernel(shifted, own, out):
    def emit(p, value):
        out[...] = value if p == 0 else out[...] + value

    half_sum(shifted, lambda pq: flipped(own, pq, 0, C), lax.axis_index("af"), emit)


def own_half(shifted, own):
    return pl.pallas_call(
        own_kernel,
        out_shape=sds((C, 1024), F32),
        compiler_params=params(20),
        cost_estimate=BRIEF,
        name="own_half",
    )(shifted, own)


def other_kernel(shifted, far, near, partial, out, total):
    core = lax.axis_index("lx") % 2

    def taps(pq):
        low = jnp.where(core == 0, far[pq].astype(F32), near[pq].astype(F32))
        high = jnp.where(core == 0, near[pq].astype(F32), far[pq].astype(F32))
        return jnp.concatenate([low, high], axis=0).astype(BF)

    def emit(p, value):
        value = value + (partial if p == 0 else total)[...]
        if p < 2:
            total[...] = value
        else:
            out[...] = value.T.astype(BF).reshape(8, 8, 16, C)

    half_sum(shifted, taps, 1 - lax.axis_index("af"), emit)


def other_half(shifted, far, near, partial):
    return pl.pallas_call(
        other_kernel,
        out_shape=sds((8, 8, 16, C), BF),
        scratch_shapes=[pltpu.VMEM((C, 1024), F32)],
        compiler_params=params(24),
        cost_estimate=BRIEF,
        name="other_half",
    )(shifted, far, near, partial)


def quarters(blocks):
    return [jnp.concatenate([v[10 * b : 10 * b + 10] for v in blocks], axis=0) for b in range(4)]


def fold_kernel(*refs):
    for stream, ins, outs in ((STREAM_A, refs[0:3], refs[6:10]), (STREAM_B, refs[3:6], refs[10:14])):
        blocks = []
        for g in range(len(stream)):
            total = ins[0][g]
            for ref in ins[1:]:
                total = total + ref[g].astype(F32)
            blocks.append(total)
        for part, ref in zip(quarters(blocks), outs):
            ref[...] = part.astype(ref.dtype)


def fold(a, b):
    outs = []
    for stream in (STREAM_A, STREAM_B):
        rows = 10 * len(stream)
        outs += [sds((rows, LANES), F32)] + [sds((rows, LANES), BF)] * 3
    return pl.pallas_call(
        fold_kernel,
        out_shape=tuple(outs),
        compiler_params=params(12),
        cost_estimate=BRIEF,
        name="fold",
    )(*a, *b)


def cut_kernel(a0, a1, a2, a3, b0, b1, b2, b3, out, s1, s2, s3):
    af = lax.axis_index("af")
    cuts = []
    for first in (af, 1 - af):
        lanes = pl.ds(pl.multiple_of(first * HALF, HALF), HALF)
        kept, given = [], []
        for refs, n in (((a0, a1, a2, a3), len(STREAM_A)), ((b0, b1, b2, b3), len(STREAM_B))):
            total = refs[0][:, lanes]
            for ref in refs[1:]:
                total = total + ref[:, lanes].astype(F32)
            for g in range(n):
                kept.append(total[10 * g : 10 * g + 5])
                given.append(total[10 * g + 5 : 10 * g + 10])
        cuts += [jnp.concatenate(kept, axis=0), jnp.concatenate(given, axis=0)]
    out[...] = cuts[0]
    s1[...] = cuts[2].astype(BF)
    s2[...] = cuts[1].astype(BF)
    s3[...] = cuts[3].astype(BF)


def cut(*operands):
    piece = sds((45, HALF), BF)
    return pl.pallas_call(
        cut_kernel,
        out_shape=(sds((45, HALF), F32), piece, piece, piece),
        compiler_params=params(),
        cost_estimate=BRIEF,
        name="cut",
    )(*operands)


def last_kernel(scale, keep, r1, r2, r3, out):
    total = (keep[...] + r1[...].astype(F32) + r2[...].astype(F32) + r3[...].astype(F32)) * scale
    for n, pq in enumerate(STREAM_A + STREAM_B):
        for r in range(3):
            out[:, 3 * pq + r, :] = total[5 * n : 5 * n + 5, 160 * r : 160 * r + 160]


def last(scale, *operands):
    return pl.pallas_call(
        functools.partial(last_kernel, scale),
        out_shape=sds((5, 27, 160), F32),
        compiler_params=params(),
        cost_estimate=BRIEF,
        name="last",
    )(*operands)


def body(grad_out, inputs, weight):
    core = lax.axis_index("lx") % 2
    scale = 1.0 / math.sqrt(16 * 64 * 128)

    grad_other = swap_core(grad_out)
    inputs_other = swap_core(inputs)
    outer = lax.dynamic_slice_in_dim(grad_out, core * 7, 1, 1).reshape(8, 16, C)
    alpha = send(outer, lambda a, b, c: ((a + 2 * (a % 2) - 1) % 8, b, c))
    quarter = flip(weight)
    alpha, grad_other, inputs_other, quarter = lax.optimization_barrier(
        (alpha, grad_other, inputs_other, quarter)
    )
    beta = swap_core(alpha)

    line, plane, corner, outer = edges(grad_out, grad_other, alpha, beta)

    def side(a, b):
        return b ^ 1 if a % 2 == 0 else (b + 2 * (b % 2) - 1) % 8

    line = send(line, lambda a, b, c: (a, side(a, b), c))
    corner = send(corner, lambda a, b, c: (a, side(a, b), c ^ 1))
    plane = send(plane, lambda a, b, c: (a, b, c ^ 1))
    turned_a, turned_b = turn(inputs, inputs_other)
    line, corner, plane, turned_a = lax.optimization_barrier((line, corner, plane, turned_a))
    line_other, corner_other, plane_other = swap_core(line), swap_core(corner), swap_core(plane)

    quarter, turned_a = lax.optimization_barrier((quarter, turned_a))
    far = send(quarter, lambda a, b, c: (a, b ^ (4 * (a % 2)), c ^ 1))

    shifted, *terms = tiles(
        grad_out, grad_other, outer,
        line, line_other, plane, plane_other, corner, corner_other, turned_a, turned_b,
    )
    a_keep, a1, a3, a_low, a_high, b_keep, b1, b3, b_low, b_high = terms
    along_z = [lambda a, b, c, s=s: (a ^ (2 * s), b, c) for s in (1, 3, 2)]
    along_x = [lambda a, b, c, s=s: (a, b ^ s, c) for s in (1, 3, 2)]
    along_y = [
        lambda a, b, c: (a, b, c ^ 1),
        lambda a, b, c: (a, b ^ 4, c),
        lambda a, b, c: (a, b ^ 4, c ^ 1),
    ]

    a_low, a_high = send(a_low, along_z[0]), send(a_high, along_z[1])
    b_low, b_high = send(b_low, along_x[0]), send(b_high, along_x[1])
    grad_input = own_half(shifted, weight)
    grad_input, far, a_low, a_high, b_low, b_high = lax.optimization_barrier(
        (grad_input, far, a_low, a_high, b_low, b_high)
    )
    near = swap_core(far)
    a1, a3, b1, b3 = join(a1, a3, a_low, a_high, b1, b3, b_low, b_high)
    a1, a3 = send(a1, along_z[0]), send(a3, along_z[1])
    b1, b3 = send(b1, along_x[0]), send(b3, along_x[1])
    grad_input = other_half(shifted, far, near, grad_input)
    grad_input, a1, a3, b1, b3 = lax.optimization_barrier((grad_input, a1, a3, b1, b3))

    both = fold((a_keep, a1, a3), (b_keep, b1, b3))
    a = [both[0]] + [send(v, to) for v, to in zip(both[1:4], along_x)]
    b = [both[4]] + [send(v, to) for v, to in zip(both[5:8], along_z)]
    keep, *outs = cut(*a, *b)
    ins = [send(v, to) for v, to in zip(outs, along_y)]
    grad_weight = last(scale, keep, *ins)
    return (grad_input, jnp.transpose(grad_weight, (1, 2, 0)))


def solution(mesh):
    placed = (P("af", "lx", "ly", None), P("af", "lx", "ly", None), P(None, "af", None))
    return jax.shard_map(
        body,
        mesh=mesh,
        in_specs=placed,
        out_specs=(P("af", "lx", "ly", None), P(None, "af", ("lx", "ly"))),
        check_vma=False,
    )
```

```python
import functools
import math

import jax
import jax.numpy as jnp
from jax import lax
from jax.experimental import pallas as pl
from jax.experimental.pallas import tpu as pltpu
from jax.sharding import PartitionSpec as P

AXES = ("lx", "ly", "af")
BF, F32 = jnp.bfloat16, jnp.float32
C = 320
HALF = 512
LANES = 2 * HALF

HALF = 512
LANES = 2 * HALF

STREAM_A = (0, 1, 2, 3, 4)
STREAM_B = (5, 6, 7, 8)


def routes(to):
    pairs = []
    for a in range(8):
        for b in range(8):
            for c in range(2):
                u, v, w = to(a, b, c)
                pairs.append(((a * 8 + b) * 2 + c, (u * 8 + v) * 2 + w))
    return pairs


def send(value, to):
    return lax.ppermute(value, AXES, routes(to))


def swap_core(v):
    return send(v, lambda a, b, c: (a ^ 1, b, c))


def params(mib=8):
    return pltpu.CompilerParams(vmem_limit_bytes=mib * 2**20)


BRIEF = pl.CostEstimate(flops=1, bytes_accessed=1, transcendentals=0)


def sds(shape, dtype):
    return jax.ShapeDtypeStruct(shape, dtype)


def edges_kernel(g, other, alpha, beta, line, half, corner, outer, plane):
    core = lax.axis_index("lx") % 2
    at = 7 - lax.axis_index("af") * 7
    column = jnp.where(lax.axis_index("ly") % 2 == core, 15, 0)

    def picker(rows, tiles):
        row = lax.broadcasted_iota(jnp.int32, (rows, 16 * tiles), 0)
        cell = lax.broadcasted_iota(jnp.int32, (rows, 16 * tiles), 1)
        return jnp.where(cell == row * 16 + column, 1.0, 0.0).astype(BF)

    pick = picker(8, 8)

    def ends(tile, to):
        got = jnp.dot(pick, tile.reshape(128, C), preferred_element_type=F32)
        line[pl.ds(to, 1)] = got.astype(BF)[None]

    for src, to in ((g, core * 8 + 1), (other, 9 - core * 8)):
        for n in range(8):
            ends(src[:, n], to + n)
        plane[pl.ds(to, 8)] = src[pl.ds(at, 1)].reshape(8, 16, C)
    z = lax.axis_index("lx") // 2
    for n, src in enumerate((alpha, beta)):
        to = 17 * (core ^ n)
        inside = jnp.where(to == 0, z > 0, z < 3)
        outer[n] = jnp.where(inside, src[...].astype(F32), 0.0).astype(BF)
        ends(outer[n], to)
        plane[pl.ds(to, 1)] = outer[n, pl.ds(at, 1)]
    half[...] = plane[pl.ds(9 * core, 9)]
    got = jnp.dot(picker(24, 18), plane[...].reshape(288, C), preferred_element_type=F32)
    corner[...] = got[:18].astype(BF)


def edges(g, other, alpha, beta):
    return pl.pallas_call(
        edges_kernel,
        out_shape=(
            sds((18, 8, C), BF),
            sds((9, 16, C), BF),
            sds((18, C), BF),
            sds((2, 8, 16, C), BF),
        ),
        scratch_shapes=[pltpu.VMEM((18, 16, C), BF)],
        compiler_params=params(10),
        cost_estimate=BRIEF,
        name="edges",
    )(g, other, alpha, beta)


def turn_kernel(own, other, out, both):
    core = lax.axis_index("lx") % 2
    mine = lax.axis_index("lx") * 8 + lax.axis_index("ly")
    both[:, pl.ds(core * 8, 8)] = own[...]
    both[:, pl.ds(8 - core * 8, 8)] = other[...]
    cells = both[...].reshape(2048, C)
    row = lax.broadcasted_iota(jnp.int32, (C, C), 0)
    fives, tens, twenties, eighties = row * 13108 >> 16, row * 6554 >> 16, row * 52429 >> 20, row * 52429 >> 22
    first, second = eighties, twenties & 3
    first, second = first ^ (first >> 1), second ^ (second >> 1)
    z, x = jnp.where(core == 0, first, second), jnp.where(core == 0, second, first)
    chunk = mine ^ (z * 16 + (tens & 1) * 8 + (fives & 1) * 4 + x)
    lane = lax.broadcasted_iota(jnp.int32, (C, C), 1)
    pick = jnp.where(lane == chunk * 5 + row - fives * 5, 1.0, 0.0).astype(BF)
    out[...] = lax.dot_general(
        pick, cells, (((1,), (1,)), ((), ())), preferred_element_type=F32
    ).astype(BF)


def turn(own, other):
    return pl.pallas_call(
        turn_kernel,
        out_shape=sds((C, 2048), BF),
        scratch_shapes=[pltpu.VMEM((8, 16, 16, C), BF)],
        compiler_params=params(12),
        cost_estimate=BRIEF,
        name="turn",
    )(own, other)


def spread(tile, left, right):
    n = tile.shape[0]
    rows = n * 16
    flat = tile.astype(F32).reshape(rows, C)
    col = lax.broadcasted_iota(jnp.int32, (n, 16, C), 1).reshape(rows, C)
    ends = jnp.broadcast_to(right.reshape(n, 1, C), (n, 16, C)).reshape(rows, C)
    heads = jnp.broadcast_to(left.reshape(n, 1, C), (n, 16, C)).reshape(rows, C)
    up = jnp.where(col == 15, ends, pltpu.roll(flat, rows - 1, 0)).astype(BF)
    down = jnp.where(col == 0, heads, pltpu.roll(flat, 1, 0)).astype(BF)
    shifts = (up, tile.reshape(rows, C), down)
    pad = jnp.zeros((rows, HALF - 480), BF)
    lanes = [v[:, :160] for v in shifts] + [pad] + [v[:, 160:] for v in shifts] + [pad]
    return jnp.concatenate(lanes, axis=1).reshape(n, 16, LANES)


def tiles_kernel(
    g, other, outer, line, line_other, half, half_other, corner, corner_other, turned,
    shifted, keep, one, three, far, plane,
):
    core = lax.axis_index("lx") % 2
    af = lax.axis_index("af")
    ly = lax.axis_index("ly")
    side = ly % 2

    def order(mine, theirs):
        mine, theirs = mine.astype(F32), theirs.astype(F32)
        left = jnp.where(side == core, theirs, mine)
        right = jnp.where(side == core, mine, theirs)
        return jnp.where(ly > 0, left, 0.0), jnp.where(ly < 7, right, 0.0)

    def put(tile, at):
        lines = order(line[pl.ds(at, 1)][0], line_other[pl.ds(at, 1)][0])
        shifted[1:9, pl.ds(at, 1)] = spread(tile, *lines)[:, None]

    for src, at in ((g, core * 8 + 1), (other, 9 - core * 8)):

        def row(n, carry, src=src, at=at):
            put(src[:, pl.ds(n, 1)].reshape(8, 16, C), at + n)
            return carry

        lax.fori_loop(0, 8, row, 0, unroll=4)
    put(outer[0], core * 17)
    put(outer[1], 17 - core * 17)
    plane[pl.ds(9 * core, 9)] = half[...]
    plane[pl.ds(9 - 9 * core, 9)] = half_other[...]
    lines = order(corner[...], corner_other[...])
    shifted[pl.ds(9 - af * 9, 1)] = spread(plane[...], *lines)[None]
    shifted[pl.ds(af * 9, 1)] = jnp.zeros((1, 18, 16, LANES), BF)
    lanes = pl.ds(pl.multiple_of(core * HALF, HALF), HALF)
    for pq in range(9):
        p, q = pq // 3, pq % 3
        cells = shifted[2 - p : 10 - p, 2 - q : 18 - q, :, lanes].reshape(2048, HALF)
        tile = jnp.dot(turned[...], cells, preferred_element_type=F32)
        keep[pq] = tile[0:80]
        for n, ref in enumerate((one, three, far)):
            ref[pq] = tile[80 * n + 80 : 80 * n + 160].astype(BF)


def tiles(*operands):
    piece = sds((9, 80, HALF), BF)
    return pl.pallas_call(
        tiles_kernel,
        out_shape=(sds((10, 18, 16, LANES), BF), sds((9, 80, HALF), F32), piece, piece, piece),
        scratch_shapes=[pltpu.VMEM((18, 16, C), BF)],
        compiler_params=params(28),
        cost_estimate=BRIEF,
        name="tiles",
    )(*operands)


def flipped(weight, pq, start, rows):
    row = lax.broadcasted_iota(jnp.int32, (rows, C), 0)
    lane = lax.broadcasted_iota(jnp.int32, (rows, C), 1)
    pick = jnp.where(lane == row + start, 1.0, 0.0).astype(BF)
    taps = weight[3 * pq : 3 * pq + 3].reshape(480, C)
    turned = lax.dot_general(pick, taps, (((1,), (1,)), ((), ())), preferred_element_type=F32)
    return jnp.concatenate([turned.astype(BF), jnp.zeros((rows, HALF - 480), BF)], axis=1)


def flip_kernel(weight, out):
    core = lax.axis_index("lx") % 2
    for pq in range(9):
        out[pq] = flipped(weight, pq, core * 160, 160)


def flip(weight):
    return pl.pallas_call(
        flip_kernel,
        out_shape=sds((9, 160, HALF), BF),
        compiler_params=params(20),
        cost_estimate=BRIEF,
        name="flip",
    )(weight)


def half_sum(shifted, taps, first, emit):
    core = lax.axis_index("lx") % 2
    lanes = pl.ds(pl.multiple_of(first * HALF, HALF), HALF)
    for p in range(3):
        value = None
        for q in range(3):
            rows = pl.ds(core * 8 + 2 - q, 8)
            cells = shifted[2 - p : 10 - p, rows, :, lanes].reshape(1024, HALF)
            term = lax.dot_general(
                taps(3 * p + q), cells, (((1,), (1,)), ((), ())), preferred_element_type=F32
            )
            value = term if value is None else value + term
        emit(p, value)


def own_kernel(shifted, own, out):
    def emit(p, value):
        out[...] = value if p == 0 else out[...] + value

    half_sum(shifted, lambda pq: flipped(own, pq, 0, C), lax.axis_index("af"), emit)


def own_half(shifted, own):
    return pl.pallas_call(
        own_kernel,
        out_shape=sds((C, 1024), F32),
        compiler_params=params(20),
        cost_estimate=BRIEF,
        name="own_half",
    )(shifted, own)


def other_kernel(shifted, far, near_low, near_high, partial, out, total):
    core = lax.axis_index("lx") % 2
    pad = jnp.zeros((160, HALF - 480), F32)

    def taps(pq):
        own = far[pq].astype(F32)
        near = jnp.concatenate([near_low[pq], near_high[pq]], axis=0).astype(F32)
        near = jnp.concatenate([near, pad], axis=1)
        low, high = jnp.where(core == 0, own, near), jnp.where(core == 0, near, own)
        return jnp.concatenate([low, high], axis=0).astype(BF)

    def emit(p, value):
        value = value + (partial if p == 0 else total)[...]
        if p < 2:
            total[...] = value
        else:
            out[...] = value.T.astype(BF).reshape(8, 8, 16, C)

    half_sum(shifted, taps, 1 - lax.axis_index("af"), emit)


def other_half(shifted, far, near, partial):
    return pl.pallas_call(
        other_kernel,
        out_shape=sds((8, 8, 16, C), BF),
        scratch_shapes=[pltpu.VMEM((C, 1024), F32)],
        compiler_params=params(24),
        cost_estimate=BRIEF,
        name="other_half",
    )(shifted, far, *near, partial)


def fold_kernel(keep, one, three, far, *outs):
    parts = [[], [], [], []]
    for pq in range(9):
        total = keep[pq]
        for ref in (one, three, far):
            total = total + ref[pq].astype(F32)
        for n in range(4):
            parts[n].append(total[20 * n : 20 * n + 20])
    for part, ref in zip(parts, outs):
        ref[...] = jnp.concatenate(part, axis=0).astype(ref.dtype)


def fold(*operands):
    piece = sds((180, HALF), BF)
    return pl.pallas_call(
        fold_kernel,
        out_shape=(sds((180, HALF), F32), piece, piece, piece),
        compiler_params=params(12),
        cost_estimate=BRIEF,
        name="fold",
    )(*operands)


def cut_kernel(keep, r1, r2, r3, out, low, high, same):
    total = keep[...]
    for ref in (r1, r2, r3):
        total = total + ref[...].astype(F32)
    tens = [total[10 * n : 10 * n + 10] for n in range(18)]
    part = jnp.concatenate([v[:5] for v in tens], axis=0)
    out[...] = part
    low[...] = part.astype(BF)
    part = jnp.concatenate([v[5:] for v in tens], axis=0).astype(BF)
    high[...] = part
    same[...] = part


def cut(*operands):
    return pl.pallas_call(
        cut_kernel,
        out_shape=(sds((90, HALF), F32),) + (sds((90, HALF), BF),) * 3,
        compiler_params=params(),
        cost_estimate=BRIEF,
        name="cut",
    )(*operands)


def close_kernel(keep, r1, r2, r3, mine, theirs):
    total = keep[...]
    for ref in (r1, r2, r3):
        total = total + ref[...].astype(F32)
    tens = [total[10 * n : 10 * n + 10] for n in range(9)]
    mine[...] = jnp.concatenate([v[:5] for v in tens], axis=0)
    theirs[...] = jnp.concatenate([v[5:] for v in tens], axis=0)


def close(*operands):
    piece = sds((45, HALF), F32)
    return pl.pallas_call(
        close_kernel,
        out_shape=(piece, piece),
        compiler_params=params(),
        cost_estimate=BRIEF,
        name="close",
    )(*operands)


def last_kernel(scale, mine, theirs, out):
    owner = lax.axis_index("af") == lax.axis_index("lx") % 2
    total = jnp.where(owner, mine[...], theirs[...]) * scale
    for pq in range(9):
        for r in range(3):
            out[:, 3 * pq + r, :] = total[5 * pq : 5 * pq + 5, 160 * r : 160 * r + 160]


def last(scale, *operands):
    return pl.pallas_call(
        functools.partial(last_kernel, scale),
        out_shape=sds((5, 27, 160), F32),
        compiler_params=params(),
        cost_estimate=BRIEF,
        name="last",
    )(*operands)


def body(grad_out, inputs, weight):
    core = lax.axis_index("lx") % 2
    scale = 1.0 / math.sqrt(16 * 64 * 128)

    grad_other = swap_core(grad_out)
    inputs_other = swap_core(inputs)
    outer = lax.dynamic_slice_in_dim(grad_out, core * 7, 1, 1).reshape(8, 16, C)
    alpha = send(outer, lambda a, b, c: ((a + 2 * (a % 2) - 1) % 8, b, c))
    quarter = flip(weight)
    alpha, grad_other, inputs_other, quarter = lax.optimization_barrier(
        (alpha, grad_other, inputs_other, quarter)
    )
    beta = swap_core(alpha)

    line, plane, corner, outer = edges(grad_out, grad_other, alpha, beta)

    def side(a, b):
        return b ^ 1 if a % 2 == 0 else (b + 2 * (b % 2) - 1) % 8

    line = send(line, lambda a, b, c: (a, side(a, b), c))
    corner = send(corner, lambda a, b, c: (a, side(a, b), c ^ 1))
    plane = send(plane, lambda a, b, c: (a, b, c ^ 1))
    turned = turn(inputs, inputs_other)
    line, corner, plane, turned = lax.optimization_barrier((line, corner, plane, turned))
    line_other, corner_other, plane_other = swap_core(line), swap_core(corner), swap_core(plane)

    quarter, turned = lax.optimization_barrier((quarter, turned))
    far = send(quarter, lambda a, b, c: (a, b ^ (4 * (a % 2)), c ^ 1))

    shifted, keep, one, three, opposite = tiles(
        grad_out, grad_other, outer,
        line, line_other, plane, plane_other, corner, corner_other, turned,
    )

    def ring(s, second):
        return lambda a, b, c: (a ^ (2 * s), b, c) if a % 2 == second else (a, b ^ s, c)

    opposite, one, three = send(opposite, ring(2, 0)), send(one, ring(1, 0)), send(three, ring(3, 0))
    grad_input = own_half(shifted, weight)
    grad_input, far = lax.optimization_barrier((grad_input, far))
    near = [swap_core(far[:, n : n + 80, :480]) for n in (0, 80)]
    grad_input = other_half(shifted, far, near, grad_input)
    grad_input, opposite, one, three = lax.optimization_barrier((grad_input, opposite, one, three))

    keep, one, three, far = fold(keep, one, three, opposite)
    far, one, three = send(far, ring(2, 1)), send(one, ring(1, 1)), send(three, ring(3, 1))
    keep, low, high, same = cut(keep, far, one, three)
    far = send(high, lambda a, b, c: (a, b ^ 4, c))
    one = send(low, lambda a, b, c: (a, b, c ^ 1))
    three = send(same, lambda a, b, c: (a, b ^ 4, c ^ 1))
    mine, theirs = close(keep, far, one, three)
    grad_weight = last(scale, mine, swap_core(theirs))
    return (grad_input, jnp.transpose(grad_weight, (1, 2, 0)))


def solution(mesh):
    placed = (P("af", "lx", "ly", None), P("af", "lx", "ly", None), P(None, "af", None))
    return jax.shard_map(
        body,
        mesh=mesh,
        in_specs=placed,
        out_specs=(P("af", "lx", "ly", None), P(None, "af", ("lx", "ly"))),
        check_vma=False,
    )
```

```python
import functools
import math

import jax
import jax.numpy as jnp
from jax import lax
from jax.experimental import pallas as pl
from jax.experimental.pallas import tpu as pltpu
from jax.sharding import PartitionSpec as P

AXES = ("lx", "ly", "af")
BF, F32 = jnp.bfloat16, jnp.float32
C = 320
HALF = 512
LANES = 2 * HALF

HALF = 512
LANES = 2 * HALF

STREAM_A = (0, 1, 2, 3, 4)
STREAM_B = (5, 6, 7, 8)


def routes(to):
    pairs = []
    for a in range(8):
        for b in range(8):
            for c in range(2):
                u, v, w = to(a, b, c)
                pairs.append(((a * 8 + b) * 2 + c, (u * 8 + v) * 2 + w))
    return pairs


def send(value, to):
    return lax.ppermute(value, AXES, routes(to))


def swap_core(v):
    return send(v, lambda a, b, c: (a ^ 1, b, c))


def params(mib=8):
    return pltpu.CompilerParams(vmem_limit_bytes=mib * 2**20)


BRIEF = pl.CostEstimate(flops=1, bytes_accessed=1, transcendentals=0)


def sds(shape, dtype):
    return jax.ShapeDtypeStruct(shape, dtype)


def edges_kernel(g, other, alpha, beta, line, half, corner, outer, plane):
    core = lax.axis_index("lx") % 2
    at = 7 - lax.axis_index("af") * 7
    column = jnp.where(lax.axis_index("ly") % 2 == core, 15, 0)

    def picker(rows, tiles):
        row = lax.broadcasted_iota(jnp.int32, (rows, 16 * tiles), 0)
        cell = lax.broadcasted_iota(jnp.int32, (rows, 16 * tiles), 1)
        return jnp.where(cell == row * 16 + column, 1.0, 0.0).astype(BF)

    pick = picker(8, 8)

    def ends(tile, to):
        got = jnp.dot(pick, tile.reshape(128, C), preferred_element_type=F32)
        line[pl.ds(to, 1)] = got.astype(BF)[None]

    for src, to in ((g, core * 8 + 1), (other, 9 - core * 8)):
        for n in range(8):
            ends(src[:, n], to + n)
        plane[pl.ds(to, 8)] = src[pl.ds(at, 1)].reshape(8, 16, C)
    z = lax.axis_index("lx") // 2
    for n, src in enumerate((alpha, beta)):
        to = 17 * (core ^ n)
        inside = jnp.where(to == 0, z > 0, z < 3)
        outer[n] = jnp.where(inside, src[...].astype(F32), 0.0).astype(BF)
        ends(outer[n], to)
        plane[pl.ds(to, 1)] = outer[n, pl.ds(at, 1)]
    half[...] = plane[pl.ds(9 * core, 9)]
    got = jnp.dot(picker(24, 18), plane[...].reshape(288, C), preferred_element_type=F32)
    corner[...] = got[:18].astype(BF)


def edges(g, other, alpha, beta):
    return pl.pallas_call(
        edges_kernel,
        out_shape=(
            sds((18, 8, C), BF),
            sds((9, 16, C), BF),
            sds((18, C), BF),
            sds((2, 8, 16, C), BF),
        ),
        scratch_shapes=[pltpu.VMEM((18, 16, C), BF)],
        compiler_params=params(10),
        cost_estimate=BRIEF,
        name="edges",
    )(g, other, alpha, beta)


def turn_kernel(own, other, out, both):
    core = lax.axis_index("lx") % 2
    mine = lax.axis_index("lx") * 8 + lax.axis_index("ly")
    both[:, pl.ds(core * 8, 8)] = own[...]
    both[:, pl.ds(8 - core * 8, 8)] = other[...]
    cells = both[...].reshape(2048, C)
    row = lax.broadcasted_iota(jnp.int32, (C, C), 0)
    fives, tens, twenties, eighties = row * 13108 >> 16, row * 6554 >> 16, row * 52429 >> 20, row * 52429 >> 22
    first, second = eighties, twenties & 3
    first, second = first ^ (first >> 1), second ^ (second >> 1)
    z, x = jnp.where(core == 0, first, second), jnp.where(core == 0, second, first)
    chunk = mine ^ (z * 16 + (tens & 1) * 8 + (fives & 1) * 4 + x)
    lane = lax.broadcasted_iota(jnp.int32, (C, C), 1)
    pick = jnp.where(lane == chunk * 5 + row - fives * 5, 1.0, 0.0).astype(BF)
    out[...] = lax.dot_general(
        pick, cells, (((1,), (1,)), ((), ())), preferred_element_type=F32
    ).astype(BF)


def turn(own, other):
    return pl.pallas_call(
        turn_kernel,
        out_shape=sds((C, 2048), BF),
        scratch_shapes=[pltpu.VMEM((8, 16, 16, C), BF)],
        compiler_params=params(12),
        cost_estimate=BRIEF,
        name="turn",
    )(own, other)


def spread(tile, left, right):
    n = tile.shape[0]
    rows = n * 16
    flat = tile.astype(F32).reshape(rows, C)
    col = lax.broadcasted_iota(jnp.int32, (n, 16, C), 1).reshape(rows, C)
    ends = jnp.broadcast_to(right.reshape(n, 1, C), (n, 16, C)).reshape(rows, C)
    heads = jnp.broadcast_to(left.reshape(n, 1, C), (n, 16, C)).reshape(rows, C)
    up = jnp.where(col == 15, ends, pltpu.roll(flat, rows - 1, 0)).astype(BF)
    down = jnp.where(col == 0, heads, pltpu.roll(flat, 1, 0)).astype(BF)
    shifts = (up, tile.reshape(rows, C), down)
    pad = jnp.zeros((rows, HALF - 480), BF)
    lanes = [v[:, :160] for v in shifts] + [pad] + [v[:, 160:] for v in shifts] + [pad]
    return jnp.concatenate(lanes, axis=1).reshape(n, 16, LANES)


def tiles_kernel(
    g, other, outer, line, line_other, half, half_other, corner, corner_other, turned,
    shifted, keep, one, three, far, plane,
):
    core = lax.axis_index("lx") % 2
    af = lax.axis_index("af")
    ly = lax.axis_index("ly")
    side = ly % 2

    def order(mine, theirs):
        mine, theirs = mine.astype(F32), theirs.astype(F32)
        left = jnp.where(side == core, theirs, mine)
        right = jnp.where(side == core, mine, theirs)
        return jnp.where(ly > 0, left, 0.0), jnp.where(ly < 7, right, 0.0)

    def put(tile, at):
        lines = order(line[pl.ds(at, 1)][0], line_other[pl.ds(at, 1)][0])
        shifted[1:9, pl.ds(at, 1)] = spread(tile, *lines)[:, None]

    for src, at in ((g, core * 8 + 1), (other, 9 - core * 8)):

        def row(n, carry, src=src, at=at):
            put(src[:, pl.ds(n, 1)].reshape(8, 16, C), at + n)
            return carry

        lax.fori_loop(0, 8, row, 0, unroll=4)
    put(outer[0], core * 17)
    put(outer[1], 17 - core * 17)
    plane[pl.ds(9 * core, 9)] = half[...]
    plane[pl.ds(9 - 9 * core, 9)] = half_other[...]
    lines = order(corner[...], corner_other[...])
    shifted[pl.ds(9 - af * 9, 1)] = spread(plane[...], *lines)[None]
    shifted[pl.ds(af * 9, 1)] = jnp.zeros((1, 18, 16, LANES), BF)
    lanes = pl.ds(pl.multiple_of(core * HALF, HALF), HALF)
    for pq in range(9):
        p, q = pq // 3, pq % 3
        cells = shifted[2 - p : 10 - p, 2 - q : 18 - q, :, lanes].reshape(2048, HALF)
        tile = jnp.dot(turned[...], cells, preferred_element_type=F32)
        keep[pq] = tile[0:80]
        for n, ref in enumerate((one, three, far)):
            ref[pq] = tile[80 * n + 80 : 80 * n + 160].astype(BF)


def tiles(*operands):
    piece = sds((9, 80, HALF), BF)
    return pl.pallas_call(
        tiles_kernel,
        out_shape=(sds((10, 18, 16, LANES), BF), sds((9, 80, HALF), F32), piece, piece, piece),
        scratch_shapes=[pltpu.VMEM((18, 16, C), BF)],
        compiler_params=params(28),
        cost_estimate=BRIEF,
        name="tiles",
    )(*operands)


def flipped(weight, pq, start, rows):
    row = lax.broadcasted_iota(jnp.int32, (rows, C), 0)
    lane = lax.broadcasted_iota(jnp.int32, (rows, C), 1)
    pick = jnp.where(lane == row + start, 1.0, 0.0).astype(BF)
    taps = weight[3 * pq : 3 * pq + 3].reshape(480, C)
    turned = lax.dot_general(pick, taps, (((1,), (1,)), ((), ())), preferred_element_type=F32)
    return jnp.concatenate([turned.astype(BF), jnp.zeros((rows, HALF - 480), BF)], axis=1)


def flip_kernel(weight, after, out):
    core = lax.axis_index("lx") % 2
    for pq in range(9):
        out[pq] = flipped(weight, pq, core * 160, 160)


def flip(weight, after):
    vmem, hbm = pl.BlockSpec(memory_space=pltpu.VMEM), pl.BlockSpec(memory_space=pl.ANY)
    return pl.pallas_call(
        flip_kernel,
        out_shape=sds((9, 160, HALF), BF),
        in_specs=[vmem, hbm],
        out_specs=vmem,
        compiler_params=params(20),
        cost_estimate=BRIEF,
        name="flip",
    )(weight, after)


def half_sum(shifted, taps, first, emit):
    core = lax.axis_index("lx") % 2
    lanes = pl.ds(pl.multiple_of(first * HALF, HALF), HALF)
    for p in range(3):
        value = None
        for q in range(3):
            rows = pl.ds(core * 8 + 2 - q, 8)
            cells = shifted[2 - p : 10 - p, rows, :, lanes].reshape(1024, HALF)
            term = lax.dot_general(
                taps(3 * p + q), cells, (((1,), (1,)), ((), ())), preferred_element_type=F32
            )
            value = term if value is None else value + term
        emit(p, value)


def own_kernel(shifted, own, out):
    def emit(p, value):
        out[...] = value if p == 0 else out[...] + value

    half_sum(shifted, lambda pq: flipped(own, pq, 0, C), lax.axis_index("af"), emit)


def own_half(shifted, own):
    return pl.pallas_call(
        own_kernel,
        out_shape=sds((C, 1024), F32),
        compiler_params=params(20),
        cost_estimate=BRIEF,
        name="own_half",
    )(shifted, own)


def other_kernel(shifted, far, near_low, near_high, partial, out, total):
    core = lax.axis_index("lx") % 2
    pad = jnp.zeros((160, HALF - 480), F32)

    def taps(pq):
        own = far[pq].astype(F32)
        near = jnp.concatenate([near_low[pq], near_high[pq]], axis=0).astype(F32)
        near = jnp.concatenate([near, pad], axis=1)
        low, high = jnp.where(core == 0, own, near), jnp.where(core == 0, near, own)
        return jnp.concatenate([low, high], axis=0).astype(BF)

    def emit(p, value):
        value = value + (partial if p == 0 else total)[...]
        if p < 2:
            total[...] = value
        else:
            out[...] = value.T.astype(BF).reshape(8, 8, 16, C)

    half_sum(shifted, taps, 1 - lax.axis_index("af"), emit)


def other_half(shifted, far, near, partial):
    return pl.pallas_call(
        other_kernel,
        out_shape=sds((8, 8, 16, C), BF),
        scratch_shapes=[pltpu.VMEM((C, 1024), F32)],
        compiler_params=params(24),
        cost_estimate=BRIEF,
        name="other_half",
    )(shifted, far, *near, partial)


def fold_kernel(keep, one, three, far, *outs):
    parts = [[], [], [], []]
    for pq in range(9):
        total = keep[pq]
        for ref in (one, three, far):
            total = total + ref[pq].astype(F32)
        for n in range(4):
            parts[n].append(total[20 * n : 20 * n + 20])
    for part, ref in zip(parts, outs):
        ref[...] = jnp.concatenate(part, axis=0).astype(ref.dtype)


def fold(*operands):
    piece = sds((180, HALF), BF)
    return pl.pallas_call(
        fold_kernel,
        out_shape=(sds((180, HALF), F32), piece, piece, piece),
        compiler_params=params(12),
        cost_estimate=BRIEF,
        name="fold",
    )(*operands)


def cut_kernel(keep, r1, r2, r3, mine, s1, s2, s3, s4):
    home = lax.axis_index("af") == lax.axis_index("lx") % 2
    total = keep[...]
    for ref in (r1, r2, r3):
        total = total + ref[...].astype(F32)
    same, far_same, other, far_other = (
        jnp.concatenate([total[20 * n + at : 20 * n + at + 5] for n in range(9)], axis=0)
        for at in (0, 5, 10, 15)
    )
    mine[...] = same
    s1[...] = jnp.where(home, other, same).astype(BF)
    s2[...] = jnp.where(home, far_other, far_same).astype(BF)
    s3[...] = jnp.where(home, far_same, other).astype(BF)
    s4[...] = far_other.astype(BF)


def cut(*operands):
    return pl.pallas_call(
        cut_kernel,
        out_shape=(sds((45, HALF), F32),) + (sds((45, HALF), BF),) * 4,
        compiler_params=params(),
        cost_estimate=BRIEF,
        name="cut",
    )(*operands)


def last_kernel(scale, mine, r1, r2, r3, r4, out):
    home = lax.axis_index("af") == lax.axis_index("lx") % 2
    total = r1[...].astype(F32) + r2[...].astype(F32) + r3[...].astype(F32)
    total = (total + jnp.where(home, mine[...], r4[...].astype(F32))) * scale
    for pq in range(9):
        for r in range(3):
            out[:, 3 * pq + r, :] = total[5 * pq : 5 * pq + 5, 160 * r : 160 * r + 160]


def last(scale, *operands):
    return pl.pallas_call(
        functools.partial(last_kernel, scale),
        out_shape=sds((5, 27, 160), F32),
        compiler_params=params(),
        cost_estimate=BRIEF,
        name="last",
    )(*operands)


def body(grad_out, inputs, weight):
    core = lax.axis_index("lx") % 2
    scale = 1.0 / math.sqrt(16 * 64 * 128)

    grad_other = swap_core(grad_out)
    inputs_other = swap_core(inputs)
    outer = lax.dynamic_slice_in_dim(grad_out, core * 7, 1, 1).reshape(8, 16, C)
    alpha = send(outer, lambda a, b, c: ((a + 2 * (a % 2) - 1) % 8, b, c))
    beta = send(outer, lambda a, b, c: ((a + 4 * (a % 2) - 2) % 8, b, c))
    turned = turn(inputs, inputs_other)
    alpha, beta, grad_other, turned = lax.optimization_barrier((alpha, beta, grad_other, turned))

    line, plane, corner, outer = edges(grad_out, grad_other, alpha, beta)
    quarter = flip(weight, corner)

    def side(a, b):
        return b ^ 1 if a % 2 == 0 else (b + 2 * (b % 2) - 1) % 8

    line = send(line, lambda a, b, c: (a, side(a, b), c))
    corner = send(corner, lambda a, b, c: (a, side(a, b), c ^ 1))
    plane = send(plane, lambda a, b, c: (a, b, c ^ 1))
    line, corner, plane, quarter = lax.optimization_barrier((line, corner, plane, quarter))
    line_other, corner_other, plane_other = swap_core(line), swap_core(corner), swap_core(plane)

    far = send(quarter, lambda a, b, c: (a, b ^ (4 * (a % 2)), c ^ 1))

    shifted, keep, one, three, opposite = tiles(
        grad_out, grad_other, outer,
        line, line_other, plane, plane_other, corner, corner_other, turned,
    )

    def ring(s, second):
        return lambda a, b, c: (a ^ (2 * s), b, c) if a % 2 == second else (a, b ^ s, c)

    opposite, one, three = send(opposite, ring(2, 0)), send(one, ring(1, 0)), send(three, ring(3, 0))
    grad_input = own_half(shifted, weight)
    grad_input, far = lax.optimization_barrier((grad_input, far))
    near = [swap_core(far[:, n : n + 80, :480]) for n in (0, 80)]
    grad_input = other_half(shifted, far, near, grad_input)
    grad_input, opposite, one, three = lax.optimization_barrier((grad_input, opposite, one, three))

    keep, one, three, far = fold(keep, one, three, opposite)
    far, one, three = send(far, ring(2, 1)), send(one, ring(1, 1)), send(three, ring(3, 1))
    mine, *sums = cut(keep, far, one, three)

    def either(home, away):
        return lambda a, b, c: home(a, b, c) if a % 2 == c else away(a, b, c)

    steps = (
        either(lambda a, b, c: (a ^ 1, b, c), lambda a, b, c: (a, b, c ^ 1)),
        either(lambda a, b, c: (a ^ 1, b ^ 4, c), lambda a, b, c: (a, b ^ 4, c ^ 1)),
        either(lambda a, b, c: (a, b ^ 4, c), lambda a, b, c: (a ^ 1, b, c ^ 1)),
        either(lambda a, b, c: (a, b, c), lambda a, b, c: (a ^ 1, b ^ 4, c ^ 1)),
    )
    sums = [send(v, to) for v, to in zip(sums, steps)]
    grad_weight = last(scale, mine, *sums)
    return (grad_input, jnp.transpose(grad_weight, (1, 2, 0)))


def solution(mesh):
    placed = (P("af", "lx", "ly", None), P("af", "lx", "ly", None), P(None, "af", None))
    return jax.shard_map(
        body,
        mesh=mesh,
        in_specs=placed,
        out_specs=(P("af", "lx", "ly", None), P(None, "af", ("lx", "ly"))),
        check_vma=False,
    )
```

```python
import functools
import math

import jax
import jax.numpy as jnp
from jax import lax
from jax.experimental import pallas as pl
from jax.experimental.pallas import tpu as pltpu
from jax.sharding import PartitionSpec as P

AXES = ("lx", "ly", "af")
BF, F32 = jnp.bfloat16, jnp.float32
C = 320
HALF = 512
LANES = 2 * HALF

HALF = 512
LANES = 2 * HALF

STREAM_A = (0, 1, 2, 3, 4)
STREAM_B = (5, 6, 7, 8)


def routes(to):
    pairs = []
    for a in range(8):
        for b in range(8):
            for c in range(2):
                u, v, w = to(a, b, c)
                pairs.append(((a * 8 + b) * 2 + c, (u * 8 + v) * 2 + w))
    return pairs


def send(value, to):
    return lax.ppermute(value, AXES, routes(to))


def swap_core(v):
    return send(v, lambda a, b, c: (a ^ 1, b, c))


def params(mib=8):
    return pltpu.CompilerParams(vmem_limit_bytes=mib * 2**20)


BRIEF = pl.CostEstimate(flops=1, bytes_accessed=1, transcendentals=0)
LONG = pl.CostEstimate(flops=4 * 10**10, bytes_accessed=10**7, transcendentals=0)


def sds(shape, dtype):
    return jax.ShapeDtypeStruct(shape, dtype)


def edges_kernel(g, other, alpha, beta, line, half, corner, outer, plane):
    core = lax.axis_index("lx") % 2
    at = 7 - lax.axis_index("af") * 7
    column = jnp.where(lax.axis_index("ly") % 2 == core, 15, 0)

    def picker(rows, tiles):
        row = lax.broadcasted_iota(jnp.int32, (rows, 16 * tiles), 0)
        cell = lax.broadcasted_iota(jnp.int32, (rows, 16 * tiles), 1)
        return jnp.where(cell == row * 16 + column, 1.0, 0.0).astype(BF)

    pick = picker(8, 8)

    def ends(tile, to):
        got = jnp.dot(pick, tile.reshape(128, C), preferred_element_type=F32)
        line[pl.ds(to, 1)] = got.astype(BF)[None]

    for src, to in ((g, core * 8 + 1), (other, 9 - core * 8)):
        for n in range(8):
            ends(src[:, n], to + n)
        plane[pl.ds(to, 8)] = src[pl.ds(at, 1)].reshape(8, 16, C)
    z = lax.axis_index("lx") // 2
    for n, src in enumerate((alpha, beta)):
        to = 17 * (core ^ n)
        inside = jnp.where(to == 0, z > 0, z < 3)
        outer[n] = jnp.where(inside, src[...].astype(F32), 0.0).astype(BF)
        ends(outer[n], to)
        plane[pl.ds(to, 1)] = outer[n, pl.ds(at, 1)]
    half[...] = plane[pl.ds(9 * core, 9)]
    got = jnp.dot(picker(24, 18), plane[...].reshape(288, C), preferred_element_type=F32)
    corner[...] = got[:18].astype(BF)


def edges(g, other, alpha, beta):
    return pl.pallas_call(
        edges_kernel,
        out_shape=(
            sds((18, 8, C), BF),
            sds((9, 16, C), BF),
            sds((18, C), BF),
            sds((2, 8, 16, C), BF),
        ),
        scratch_shapes=[pltpu.VMEM((18, 16, C), BF)],
        compiler_params=params(10),
        cost_estimate=BRIEF,
        name="edges",
    )(g, other, alpha, beta)


def turn_kernel(own, other, out, both):
    core = lax.axis_index("lx") % 2
    mine = lax.axis_index("lx") * 8 + lax.axis_index("ly")
    both[:, pl.ds(core * 8, 8)] = own[...]
    both[:, pl.ds(8 - core * 8, 8)] = other[...]
    cells = both[...].reshape(2048, C)
    row = lax.broadcasted_iota(jnp.int32, (C, C), 0)
    fives, tens, twenties, eighties = row * 13108 >> 16, row * 6554 >> 16, row * 52429 >> 20, row * 52429 >> 22
    first, second = eighties, twenties & 3
    first, second = first ^ (first >> 1), second ^ (second >> 1)
    z, x = jnp.where(core == 0, first, second), jnp.where(core == 0, second, first)
    chunk = mine ^ (z * 16 + (tens & 1) * 8 + (fives & 1) * 4 + x)
    lane = lax.broadcasted_iota(jnp.int32, (C, C), 1)
    pick = jnp.where(lane == chunk * 5 + row - fives * 5, 1.0, 0.0).astype(BF)
    out[...] = lax.dot_general(
        pick, cells, (((1,), (1,)), ((), ())), preferred_element_type=F32
    ).astype(BF)


def turn(own, other):
    return pl.pallas_call(
        turn_kernel,
        out_shape=sds((C, 2048), BF),
        scratch_shapes=[pltpu.VMEM((8, 16, 16, C), BF)],
        compiler_params=params(12),
        cost_estimate=BRIEF,
        name="turn",
    )(own, other)


def spread(tile, left, right):
    n = tile.shape[0]
    rows = n * 16
    flat = tile.astype(F32).reshape(rows, C)
    col = lax.broadcasted_iota(jnp.int32, (n, 16, C), 1).reshape(rows, C)
    ends = jnp.broadcast_to(right.reshape(n, 1, C), (n, 16, C)).reshape(rows, C)
    heads = jnp.broadcast_to(left.reshape(n, 1, C), (n, 16, C)).reshape(rows, C)
    up = jnp.where(col == 15, ends, pltpu.roll(flat, rows - 1, 0)).astype(BF)
    down = jnp.where(col == 0, heads, pltpu.roll(flat, 1, 0)).astype(BF)
    shifts = (up, tile.reshape(rows, C), down)
    pad = jnp.zeros((rows, HALF - 480), BF)
    lanes = [v[:, :160] for v in shifts] + [pad] + [v[:, 160:] for v in shifts] + [pad]
    return jnp.concatenate(lanes, axis=1).reshape(n, 16, LANES)


def tiles_kernel(
    g, other, outer, line, line_other, half, half_other, corner, corner_other, turned,
    shifted, keep, one, three, far, plane,
):
    core = lax.axis_index("lx") % 2
    af = lax.axis_index("af")
    ly = lax.axis_index("ly")
    side = ly % 2

    def order(mine, theirs):
        mine, theirs = mine.astype(F32), theirs.astype(F32)
        left = jnp.where(side == core, theirs, mine)
        right = jnp.where(side == core, mine, theirs)
        return jnp.where(ly > 0, left, 0.0), jnp.where(ly < 7, right, 0.0)

    def put(tile, at):
        lines = order(line[pl.ds(at, 1)][0], line_other[pl.ds(at, 1)][0])
        shifted[1:9, pl.ds(at, 1)] = spread(tile, *lines)[:, None]

    for src, at in ((g, core * 8 + 1), (other, 9 - core * 8)):

        def row(n, carry, src=src, at=at):
            put(src[:, pl.ds(n, 1)].reshape(8, 16, C), at + n)
            return carry

        lax.fori_loop(0, 8, row, 0, unroll=4)
    put(outer[0], core * 17)
    put(outer[1], 17 - core * 17)
    plane[pl.ds(9 * core, 9)] = half[...]
    plane[pl.ds(9 - 9 * core, 9)] = half_other[...]
    lines = order(corner[...], corner_other[...])
    shifted[pl.ds(9 - af * 9, 1)] = spread(plane[...], *lines)[None]
    shifted[pl.ds(af * 9, 1)] = jnp.zeros((1, 18, 16, LANES), BF)
    lanes = pl.ds(pl.multiple_of(core * HALF, HALF), HALF)
    for pq in range(9):
        p, q = pq // 3, pq % 3
        cells = shifted[2 - p : 10 - p, 2 - q : 18 - q, :, lanes].reshape(2048, HALF)
        tile = jnp.dot(turned[...], cells, preferred_element_type=F32)
        keep[pq] = tile[0:80]
        for n, ref in enumerate((one, three, far)):
            ref[pq] = tile[80 * n + 80 : 80 * n + 160].astype(BF)


def tiles(*operands):
    piece = sds((9, 80, HALF), BF)
    return pl.pallas_call(
        tiles_kernel,
        out_shape=(sds((10, 18, 16, LANES), BF), sds((9, 80, HALF), F32), piece, piece, piece),
        scratch_shapes=[pltpu.VMEM((18, 16, C), BF)],
        compiler_params=params(28),
        cost_estimate=LONG,
        name="tiles",
    )(*operands)


def flipped(weight, pq, start, rows):
    row = lax.broadcasted_iota(jnp.int32, (rows, C), 0)
    lane = lax.broadcasted_iota(jnp.int32, (rows, C), 1)
    pick = jnp.where(lane == row + start, 1.0, 0.0).astype(BF)
    taps = weight[3 * pq : 3 * pq + 3].reshape(480, C)
    turned = lax.dot_general(pick, taps, (((1,), (1,)), ((), ())), preferred_element_type=F32)
    return jnp.concatenate([turned.astype(BF), jnp.zeros((rows, HALF - 480), BF)], axis=1)


def flip_kernel(weight, after, out):
    core = lax.axis_index("lx") % 2
    for pq in range(9):
        out[pq] = flipped(weight, pq, core * 160, 160)


def flip(weight, after):
    vmem, hbm = pl.BlockSpec(memory_space=pltpu.VMEM), pl.BlockSpec(memory_space=pl.ANY)
    return pl.pallas_call(
        flip_kernel,
        out_shape=sds((9, 160, HALF), BF),
        in_specs=[vmem, hbm],
        out_specs=vmem,
        compiler_params=params(20),
        cost_estimate=BRIEF,
        name="flip",
    )(weight, after)


def half_sum(shifted, taps, first, emit):
    core = lax.axis_index("lx") % 2
    lanes = pl.ds(pl.multiple_of(first * HALF, HALF), HALF)
    for p in range(3):
        value = None
        for q in range(3):
            rows = pl.ds(core * 8 + 2 - q, 8)
            cells = shifted[2 - p : 10 - p, rows, :, lanes].reshape(1024, HALF)
            term = lax.dot_general(
                taps(3 * p + q), cells, (((1,), (1,)), ((), ())), preferred_element_type=F32
            )
            value = term if value is None else value + term
        emit(p, value)


def own_kernel(shifted, own, out):
    def emit(p, value):
        out[...] = value if p == 0 else out[...] + value

    half_sum(shifted, lambda pq: flipped(own, pq, 0, C), lax.axis_index("af"), emit)


def own_half(shifted, own):
    return pl.pallas_call(
        own_kernel,
        out_shape=sds((C, 1024), F32),
        compiler_params=params(20),
        cost_estimate=BRIEF,
        name="own_half",
    )(shifted, own)


def other_kernel(shifted, far, near_low, near_high, partial, out, total):
    core = lax.axis_index("lx") % 2
    pad = jnp.zeros((160, HALF - 480), F32)

    def taps(pq):
        own = far[pq].astype(F32)
        near = jnp.concatenate([near_low[pq], near_high[pq]], axis=0).astype(F32)
        near = jnp.concatenate([near, pad], axis=1)
        low, high = jnp.where(core == 0, own, near), jnp.where(core == 0, near, own)
        return jnp.concatenate([low, high], axis=0).astype(BF)

    def emit(p, value):
        value = value + (partial if p == 0 else total)[...]
        if p < 2:
            total[...] = value
        else:
            out[...] = value.T.astype(BF).reshape(8, 8, 16, C)

    half_sum(shifted, taps, 1 - lax.axis_index("af"), emit)


def other_half(shifted, far, near, partial):
    return pl.pallas_call(
        other_kernel,
        out_shape=sds((8, 8, 16, C), BF),
        scratch_shapes=[pltpu.VMEM((C, 1024), F32)],
        compiler_params=params(24),
        cost_estimate=BRIEF,
        name="other_half",
    )(shifted, far, *near, partial)


def fold_kernel(keep, one, three, far, *outs):
    parts = [[], [], [], []]
    for pq in range(9):
        total = keep[pq]
        for ref in (one, three, far):
            total = total + ref[pq].astype(F32)
        for n in range(4):
            parts[n].append(total[20 * n : 20 * n + 20])
    for part, ref in zip(parts, outs):
        ref[...] = jnp.concatenate(part, axis=0).astype(ref.dtype)


def fold(*operands):
    piece = sds((180, HALF), BF)
    return pl.pallas_call(
        fold_kernel,
        out_shape=(sds((180, HALF), F32), piece, piece, piece),
        compiler_params=params(12),
        cost_estimate=BRIEF,
        name="fold",
    )(*operands)


def cut_kernel(keep, r1, r2, r3, mine, s1, s2, s3, s4):
    home = lax.axis_index("af") == lax.axis_index("lx") % 2
    total = keep[...]
    for ref in (r1, r2, r3):
        total = total + ref[...].astype(F32)
    same, far_same, other, far_other = (
        jnp.concatenate([total[20 * n + at : 20 * n + at + 5] for n in range(9)], axis=0)
        for at in (0, 5, 10, 15)
    )
    mine[...] = same
    s1[...] = jnp.where(home, other, same).astype(BF)
    s2[...] = jnp.where(home, far_other, far_same).astype(BF)
    s3[...] = jnp.where(home, far_same, other).astype(BF)
    s4[...] = far_other.astype(BF)


def cut(*operands):
    return pl.pallas_call(
        cut_kernel,
        out_shape=(sds((45, HALF), F32),) + (sds((45, HALF), BF),) * 4,
        compiler_params=params(),
        cost_estimate=BRIEF,
        name="cut",
    )(*operands)


def last_kernel(scale, mine, r1, r2, r3, r4, out):
    home = lax.axis_index("af") == lax.axis_index("lx") % 2
    total = r1[...].astype(F32) + r2[...].astype(F32) + r3[...].astype(F32)
    total = (total + jnp.where(home, mine[...], r4[...].astype(F32))) * scale
    for pq in range(9):
        for r in range(3):
            out[:, 3 * pq + r, :] = total[5 * pq : 5 * pq + 5, 160 * r : 160 * r + 160]


def last(scale, *operands):
    return pl.pallas_call(
        functools.partial(last_kernel, scale),
        out_shape=sds((5, 27, 160), F32),
        compiler_params=params(),
        cost_estimate=BRIEF,
        name="last",
    )(*operands)


def body(grad_out, inputs, weight):
    core = lax.axis_index("lx") % 2
    scale = 1.0 / math.sqrt(16 * 64 * 128)

    grad_other = swap_core(grad_out)
    inputs_other = swap_core(inputs)
    outer = lax.dynamic_slice_in_dim(grad_out, core * 7, 1, 1).reshape(8, 16, C)
    alpha = send(outer, lambda a, b, c: ((a + 2 * (a % 2) - 1) % 8, b, c))
    beta = send(outer, lambda a, b, c: ((a + 4 * (a % 2) - 2) % 8, b, c))
    turned = turn(inputs, inputs_other)
    alpha, beta, grad_other, turned = lax.optimization_barrier((alpha, beta, grad_other, turned))

    line, plane, corner, outer = edges(grad_out, grad_other, alpha, beta)
    quarter = flip(weight, corner)

    def side(a, b):
        return b ^ 1 if a % 2 == 0 else (b + 2 * (b % 2) - 1) % 8

    line = send(line, lambda a, b, c: (a, side(a, b), c))
    corner = send(corner, lambda a, b, c: (a, side(a, b), c ^ 1))
    plane = send(plane, lambda a, b, c: (a, b, c ^ 1))
    line, corner, plane, quarter = lax.optimization_barrier((line, corner, plane, quarter))
    line_other, corner_other, plane_other = swap_core(line), swap_core(corner), swap_core(plane)

    far = send(quarter, lambda a, b, c: (a, b ^ (4 * (a % 2)), c ^ 1))

    shifted, keep, one, three, opposite = tiles(
        grad_out, grad_other, outer,
        line, line_other, plane, plane_other, corner, corner_other, turned,
    )

    def ring(s, second):
        return lambda a, b, c: (a ^ (2 * s), b, c) if a % 2 == second else (a, b ^ s, c)

    opposite, one, three = send(opposite, ring(2, 0)), send(one, ring(1, 0)), send(three, ring(3, 0))
    grad_input = own_half(shifted, weight)
    grad_input, far = lax.optimization_barrier((grad_input, far))
    near = [swap_core(far[:, n : n + 80, :480]) for n in (0, 80)]
    grad_input = other_half(shifted, far, near, grad_input)
    grad_input, opposite, one, three = lax.optimization_barrier((grad_input, opposite, one, three))

    keep, one, three, far = fold(keep, one, three, opposite)
    far, one, three = send(far, ring(2, 1)), send(one, ring(1, 1)), send(three, ring(3, 1))
    mine, *sums = cut(keep, far, one, three)

    def either(home, away):
        return lambda a, b, c: home(a, b, c) if a % 2 == c else away(a, b, c)

    steps = (
        either(lambda a, b, c: (a ^ 1, b, c), lambda a, b, c: (a, b, c ^ 1)),
        either(lambda a, b, c: (a ^ 1, b ^ 4, c), lambda a, b, c: (a, b ^ 4, c ^ 1)),
        either(lambda a, b, c: (a, b ^ 4, c), lambda a, b, c: (a ^ 1, b, c ^ 1)),
        either(lambda a, b, c: (a, b, c), lambda a, b, c: (a ^ 1, b ^ 4, c ^ 1)),
    )
    sums = [send(v, to) for v, to in zip(sums, steps)]
    grad_weight = last(scale, mine, *sums)
    return (grad_input, jnp.transpose(grad_weight, (1, 2, 0)))


def solution(mesh):
    placed = (P("af", "lx", "ly", None), P("af", "lx", "ly", None), P(None, "af", None))
    return jax.shard_map(
        body,
        mesh=mesh,
        in_specs=placed,
        out_specs=(P("af", "lx", "ly", None), P(None, "af", ("lx", "ly"))),
        check_vma=False,
    )
```

```python
import functools
import math

import jax
import jax.numpy as jnp
from jax import lax
from jax.experimental import pallas as pl
from jax.experimental.pallas import tpu as pltpu
from jax.sharding import PartitionSpec as P

AXES = ("lx", "ly", "af")
BF, F32 = jnp.bfloat16, jnp.float32
C = 320
HALF = 512
LANES = 2 * HALF

HALF = 512
LANES = 2 * HALF

STREAM_A = (0, 1, 2, 3, 4)
STREAM_B = (5, 6, 7, 8)


def routes(to):
    pairs = []
    for a in range(8):
        for b in range(8):
            for c in range(2):
                u, v, w = to(a, b, c)
                pairs.append(((a * 8 + b) * 2 + c, (u * 8 + v) * 2 + w))
    return pairs


def send(value, to):
    return lax.ppermute(value, AXES, routes(to))


def swap_core(v):
    return send(v, lambda a, b, c: (a ^ 1, b, c))


def params(mib=8):
    return pltpu.CompilerParams(vmem_limit_bytes=mib * 2**20)


BRIEF = pl.CostEstimate(flops=1, bytes_accessed=1, transcendentals=0)
LONG = pl.CostEstimate(flops=4 * 10**10, bytes_accessed=10**7, transcendentals=0)


def sds(shape, dtype):
    return jax.ShapeDtypeStruct(shape, dtype)


def edges_kernel(g, other, alpha, beta, line, half, corner, outer, plane):
    core = lax.axis_index("lx") % 2
    at = 7 - lax.axis_index("af") * 7
    column = jnp.where(lax.axis_index("ly") % 2 == core, 15, 0)

    def picker(rows, tiles):
        row = lax.broadcasted_iota(jnp.int32, (rows, 16 * tiles), 0)
        cell = lax.broadcasted_iota(jnp.int32, (rows, 16 * tiles), 1)
        return jnp.where(cell == row * 16 + column, 1.0, 0.0).astype(BF)

    pick = picker(8, 8)

    def ends(tile, to):
        got = jnp.dot(pick, tile.reshape(128, C), preferred_element_type=F32)
        line[pl.ds(to, 1)] = got.astype(BF)[None]

    for src, to in ((g, core * 8 + 1), (other, 9 - core * 8)):
        for n in range(8):
            ends(src[:, n], to + n)
        plane[pl.ds(to, 8)] = src[pl.ds(at, 1)].reshape(8, 16, C)
    z = lax.axis_index("lx") // 2
    for n, src in enumerate((alpha, beta)):
        to = 17 * (core ^ n)
        inside = jnp.where(to == 0, z > 0, z < 3)
        outer[n] = jnp.where(inside, src[...].astype(F32), 0.0).astype(BF)
        ends(outer[n], to)
        plane[pl.ds(to, 1)] = outer[n, pl.ds(at, 1)]
    half[...] = plane[pl.ds(9 * core, 9)]
    got = jnp.dot(picker(24, 18), plane[...].reshape(288, C), preferred_element_type=F32)
    corner[...] = got[:18].astype(BF)


def edges(g, other, alpha, beta):
    return pl.pallas_call(
        edges_kernel,
        out_shape=(
            sds((18, 8, C), BF),
            sds((9, 16, C), BF),
            sds((18, C), BF),
            sds((2, 8, 16, C), BF),
        ),
        scratch_shapes=[pltpu.VMEM((18, 16, C), BF)],
        compiler_params=params(10),
        cost_estimate=BRIEF,
        name="edges",
    )(g, other, alpha, beta)


def turn_kernel(own, other, out, both):
    core = lax.axis_index("lx") % 2
    mine = lax.axis_index("lx") * 8 + lax.axis_index("ly")
    both[:, pl.ds(core * 8, 8)] = own[...]
    both[:, pl.ds(8 - core * 8, 8)] = other[...]
    cells = both[...].reshape(2048, C)
    row = lax.broadcasted_iota(jnp.int32, (C, C), 0)
    fives, tens, twenties, eighties = row * 13108 >> 16, row * 6554 >> 16, row * 52429 >> 20, row * 52429 >> 22
    first, second = eighties, twenties & 3
    first, second = first ^ (first >> 1), second ^ (second >> 1)
    z, x = jnp.where(core == 0, first, second), jnp.where(core == 0, second, first)
    chunk = mine ^ (z * 16 + (tens & 1) * 8 + (fives & 1) * 4 + x)
    lane = lax.broadcasted_iota(jnp.int32, (C, C), 1)
    pick = jnp.where(lane == chunk * 5 + row - fives * 5, 1.0, 0.0).astype(BF)
    out[...] = lax.dot_general(
        pick, cells, (((1,), (1,)), ((), ())), preferred_element_type=F32
    ).astype(BF)


def turn(own, other):
    return pl.pallas_call(
        turn_kernel,
        out_shape=sds((C, 2048), BF),
        scratch_shapes=[pltpu.VMEM((8, 16, 16, C), BF)],
        compiler_params=params(12),
        cost_estimate=LONG,
        name="turn",
    )(own, other)


def spread(tile, left, right):
    n = tile.shape[0]
    rows = n * 16
    flat = tile.astype(F32).reshape(rows, C)
    col = lax.broadcasted_iota(jnp.int32, (n, 16, C), 1).reshape(rows, C)
    ends = jnp.broadcast_to(right.reshape(n, 1, C), (n, 16, C)).reshape(rows, C)
    heads = jnp.broadcast_to(left.reshape(n, 1, C), (n, 16, C)).reshape(rows, C)
    up = jnp.where(col == 15, ends, pltpu.roll(flat, rows - 1, 0)).astype(BF)
    down = jnp.where(col == 0, heads, pltpu.roll(flat, 1, 0)).astype(BF)
    shifts = (up, tile.reshape(rows, C), down)
    pad = jnp.zeros((rows, HALF - 480), BF)
    lanes = [v[:, :160] for v in shifts] + [pad] + [v[:, 160:] for v in shifts] + [pad]
    return jnp.concatenate(lanes, axis=1).reshape(n, 16, LANES)


def tiles_kernel(
    g, other, outer, line, line_other, half, half_other, corner, corner_other, turned,
    shifted, keep, one, three, far, plane,
):
    core = lax.axis_index("lx") % 2
    af = lax.axis_index("af")
    ly = lax.axis_index("ly")
    side = ly % 2

    def order(mine, theirs):
        mine, theirs = mine.astype(F32), theirs.astype(F32)
        left = jnp.where(side == core, theirs, mine)
        right = jnp.where(side == core, mine, theirs)
        return jnp.where(ly > 0, left, 0.0), jnp.where(ly < 7, right, 0.0)

    def put(tile, at):
        lines = order(line[pl.ds(at, 1)][0], line_other[pl.ds(at, 1)][0])
        shifted[1:9, pl.ds(at, 1)] = spread(tile, *lines)[:, None]

    for src, at in ((g, core * 8 + 1), (other, 9 - core * 8)):

        def row(n, carry, src=src, at=at):
            put(src[:, pl.ds(n, 1)].reshape(8, 16, C), at + n)
            return carry

        lax.fori_loop(0, 8, row, 0, unroll=8)
    put(outer[0], core * 17)
    put(outer[1], 17 - core * 17)
    plane[pl.ds(9 * core, 9)] = half[...]
    plane[pl.ds(9 - 9 * core, 9)] = half_other[...]
    lines = order(corner[...], corner_other[...])
    shifted[pl.ds(9 - af * 9, 1)] = spread(plane[...], *lines)[None]
    shifted[pl.ds(af * 9, 1)] = jnp.zeros((1, 18, 16, LANES), BF)
    lanes = pl.ds(pl.multiple_of(core * HALF, HALF), HALF)
    for pq in range(9):
        p, q = pq // 3, pq % 3
        cells = shifted[2 - p : 10 - p, 2 - q : 18 - q, :, lanes].reshape(2048, HALF)
        tile = jnp.dot(turned[...], cells, preferred_element_type=F32)
        keep[pq] = tile[0:80]
        for n, ref in enumerate((one, three, far)):
            ref[pq] = tile[80 * n + 80 : 80 * n + 160].astype(BF)


def tiles(*operands):
    piece = sds((9, 80, HALF), BF)
    return pl.pallas_call(
        tiles_kernel,
        out_shape=(sds((10, 18, 16, LANES), BF), sds((9, 80, HALF), F32), piece, piece, piece),
        scratch_shapes=[pltpu.VMEM((18, 16, C), BF)],
        compiler_params=params(28),
        cost_estimate=LONG,
        name="tiles",
    )(*operands)


def flipped(weight, pq, start, rows):
    row = lax.broadcasted_iota(jnp.int32, (rows, C), 0)
    lane = lax.broadcasted_iota(jnp.int32, (rows, C), 1)
    pick = jnp.where(lane == row + start, 1.0, 0.0).astype(BF)
    taps = weight[3 * pq : 3 * pq + 3].reshape(480, C)
    turned = lax.dot_general(pick, taps, (((1,), (1,)), ((), ())), preferred_element_type=F32)
    return jnp.concatenate([turned.astype(BF), jnp.zeros((rows, HALF - 480), BF)], axis=1)


def flip_kernel(weight, after, out):
    core = lax.axis_index("lx") % 2
    for pq in range(9):
        out[pq] = flipped(weight, pq, core * 160, 160)


def flip(weight, after):
    vmem, hbm = pl.BlockSpec(memory_space=pltpu.VMEM), pl.BlockSpec(memory_space=pl.ANY)
    return pl.pallas_call(
        flip_kernel,
        out_shape=sds((9, 160, HALF), BF),
        in_specs=[vmem, hbm],
        out_specs=vmem,
        compiler_params=params(20),
        cost_estimate=BRIEF,
        name="flip",
    )(weight, after)


def half_sum(shifted, taps, first, emit):
    core = lax.axis_index("lx") % 2
    lanes = pl.ds(pl.multiple_of(first * HALF, HALF), HALF)
    for p in range(3):
        value = None
        for q in range(3):
            rows = pl.ds(core * 8 + 2 - q, 8)
            cells = shifted[2 - p : 10 - p, rows, :, lanes].reshape(1024, HALF)
            term = lax.dot_general(
                taps(3 * p + q), cells, (((1,), (1,)), ((), ())), preferred_element_type=F32
            )
            value = term if value is None else value + term
        emit(p, value)


def own_kernel(shifted, own, out):
    def emit(p, value):
        out[...] = value if p == 0 else out[...] + value

    half_sum(shifted, lambda pq: flipped(own, pq, 0, C), lax.axis_index("af"), emit)


def own_half(shifted, own):
    return pl.pallas_call(
        own_kernel,
        out_shape=sds((C, 1024), F32),
        compiler_params=params(20),
        cost_estimate=BRIEF,
        name="own_half",
    )(shifted, own)


def other_kernel(shifted, far, near_low, near_high, partial, out, total):
    core = lax.axis_index("lx") % 2
    pad = jnp.zeros((160, HALF - 480), F32)

    def taps(pq):
        own = far[pq].astype(F32)
        near = jnp.concatenate([near_low[pq], near_high[pq]], axis=0).astype(F32)
        near = jnp.concatenate([near, pad], axis=1)
        low, high = jnp.where(core == 0, own, near), jnp.where(core == 0, near, own)
        return jnp.concatenate([low, high], axis=0).astype(BF)

    def emit(p, value):
        value = value + (partial if p == 0 else total)[...]
        if p < 2:
            total[...] = value
        else:
            out[...] = value.T.astype(BF).reshape(8, 8, 16, C)

    half_sum(shifted, taps, 1 - lax.axis_index("af"), emit)


def other_half(shifted, far, near, partial):
    return pl.pallas_call(
        other_kernel,
        out_shape=sds((8, 8, 16, C), BF),
        scratch_shapes=[pltpu.VMEM((C, 1024), F32)],
        compiler_params=params(24),
        cost_estimate=BRIEF,
        name="other_half",
    )(shifted, far, *near, partial)


def fold_kernel(keep, one, three, far, *outs):
    parts = [[], [], [], []]
    for pq in range(9):
        total = keep[pq]
        for ref in (one, three, far):
            total = total + ref[pq].astype(F32)
        for n in range(4):
            parts[n].append(total[20 * n : 20 * n + 20])
    for part, ref in zip(parts, outs):
        ref[...] = jnp.concatenate(part, axis=0).astype(ref.dtype)


def fold(*operands):
    piece = sds((180, HALF), BF)
    return pl.pallas_call(
        fold_kernel,
        out_shape=(sds((180, HALF), F32), piece, piece, piece),
        compiler_params=params(12),
        cost_estimate=BRIEF,
        name="fold",
    )(*operands)


def cut_kernel(keep, r1, r2, r3, mine, s1, s2, s3, s4):
    home = lax.axis_index("af") == lax.axis_index("lx") % 2
    total = keep[...]
    for ref in (r1, r2, r3):
        total = total + ref[...].astype(F32)
    same, far_same, other, far_other = (
        jnp.concatenate([total[20 * n + at : 20 * n + at + 5] for n in range(9)], axis=0)
        for at in (0, 5, 10, 15)
    )
    mine[...] = same
    s1[...] = jnp.where(home, other, same).astype(BF)
    s2[...] = jnp.where(home, far_other, far_same).astype(BF)
    s3[...] = jnp.where(home, far_same, other).astype(BF)
    s4[...] = far_other.astype(BF)


def cut(*operands):
    return pl.pallas_call(
        cut_kernel,
        out_shape=(sds((45, HALF), F32),) + (sds((45, HALF), BF),) * 4,
        compiler_params=params(),
        cost_estimate=BRIEF,
        name="cut",
    )(*operands)


def last_kernel(scale, mine, r1, r2, r3, r4, out):
    home = lax.axis_index("af") == lax.axis_index("lx") % 2
    total = r1[...].astype(F32) + r2[...].astype(F32) + r3[...].astype(F32)
    total = (total + jnp.where(home, mine[...], r4[...].astype(F32))) * scale
    for pq in range(9):
        for r in range(3):
            out[:, 3 * pq + r, :] = total[5 * pq : 5 * pq + 5, 160 * r : 160 * r + 160]


def last(scale, *operands):
    return pl.pallas_call(
        functools.partial(last_kernel, scale),
        out_shape=sds((5, 27, 160), F32),
        compiler_params=params(),
        cost_estimate=BRIEF,
        name="last",
    )(*operands)


def body(grad_out, inputs, weight):
    core = lax.axis_index("lx") % 2
    scale = 1.0 / math.sqrt(16 * 64 * 128)

    grad_other = swap_core(grad_out)
    inputs_other = swap_core(inputs)
    outer = lax.dynamic_slice_in_dim(grad_out, core * 7, 1, 1).reshape(8, 16, C)
    alpha = send(outer, lambda a, b, c: ((a + 2 * (a % 2) - 1) % 8, b, c))
    beta = send(outer, lambda a, b, c: ((a + 4 * (a % 2) - 2) % 8, b, c))
    turned = turn(inputs, inputs_other)
    alpha, beta, grad_other, turned = lax.optimization_barrier((alpha, beta, grad_other, turned))

    line, plane, corner, outer = edges(grad_out, grad_other, alpha, beta)
    quarter = flip(weight, corner)

    def side(a, b):
        return b ^ 1 if a % 2 == 0 else (b + 2 * (b % 2) - 1) % 8

    line = send(line, lambda a, b, c: (a, side(a, b), c))
    corner = send(corner, lambda a, b, c: (a, side(a, b), c ^ 1))
    plane = send(plane, lambda a, b, c: (a, b, c ^ 1))
    line, corner, plane, quarter = lax.optimization_barrier((line, corner, plane, quarter))
    line_other, corner_other, plane_other = swap_core(line), swap_core(corner), swap_core(plane)

    far = send(quarter, lambda a, b, c: (a, b ^ (4 * (a % 2)), c ^ 1))

    shifted, keep, one, three, opposite = tiles(
        grad_out, grad_other, outer,
        line, line_other, plane, plane_other, corner, corner_other, turned,
    )

    def ring(s, second):
        return lambda a, b, c: (a ^ (2 * s), b, c) if a % 2 == second else (a, b ^ s, c)

    opposite, one, three = send(opposite, ring(2, 0)), send(one, ring(1, 0)), send(three, ring(3, 0))
    grad_input = own_half(shifted, weight)
    grad_input, far = lax.optimization_barrier((grad_input, far))
    near = [swap_core(far[:, n : n + 80, :480]) for n in (0, 80)]
    grad_input = other_half(shifted, far, near, grad_input)
    grad_input, opposite, one, three = lax.optimization_barrier((grad_input, opposite, one, three))

    keep, one, three, far = fold(keep, one, three, opposite)
    far, one, three = send(far, ring(2, 1)), send(one, ring(1, 1)), send(three, ring(3, 1))
    mine, *sums = cut(keep, far, one, three)

    def either(home, away):
        return lambda a, b, c: home(a, b, c) if a % 2 == c else away(a, b, c)

    steps = (
        either(lambda a, b, c: (a ^ 1, b, c), lambda a, b, c: (a, b, c ^ 1)),
        either(lambda a, b, c: (a ^ 1, b ^ 4, c), lambda a, b, c: (a, b ^ 4, c ^ 1)),
        either(lambda a, b, c: (a, b ^ 4, c), lambda a, b, c: (a ^ 1, b, c ^ 1)),
        either(lambda a, b, c: (a, b, c), lambda a, b, c: (a ^ 1, b ^ 4, c ^ 1)),
    )
    sums = [send(sums[n], steps[n]) for n in (2, 1, 0, 3)]
    grad_weight = last(scale, mine, *sums)
    return (grad_input, jnp.transpose(grad_weight, (1, 2, 0)))


def solution(mesh):
    placed = (P("af", "lx", "ly", None), P("af", "lx", "ly", None), P(None, "af", None))
    return jax.shard_map(
        body,
        mesh=mesh,
        in_specs=placed,
        out_specs=(P("af", "lx", "ly", None), P(None, "af", ("lx", "ly"))),
        check_vma=False,
    )
```

```python
import functools
import math

import jax
import jax.numpy as jnp
from jax import lax
from jax.experimental import pallas as pl
from jax.experimental.pallas import tpu as pltpu
from jax.sharding import PartitionSpec as P

AXES = ("lx", "ly", "af")
BF, F32 = jnp.bfloat16, jnp.float32
C = 320
HALF = 512
LANES = 2 * HALF

HALF = 512
LANES = 2 * HALF

STREAM_A = (0, 1, 2, 3, 4)
STREAM_B = (5, 6, 7, 8)


def routes(to):
    pairs = []
    for a in range(8):
        for b in range(8):
            for c in range(2):
                u, v, w = to(a, b, c)
                pairs.append(((a * 8 + b) * 2 + c, (u * 8 + v) * 2 + w))
    return pairs


def send(value, to):
    return lax.ppermute(value, AXES, routes(to))


def swap_core(v):
    return send(v, lambda a, b, c: (a ^ 1, b, c))


def params(mib=8):
    return pltpu.CompilerParams(vmem_limit_bytes=mib * 2**20)


BRIEF = pl.CostEstimate(flops=1, bytes_accessed=1, transcendentals=0)
LONG = pl.CostEstimate(flops=4 * 10**10, bytes_accessed=10**7, transcendentals=0)


def sds(shape, dtype):
    return jax.ShapeDtypeStruct(shape, dtype)


def edges_kernel(g, other, alpha, beta, line, half, corner, outer, plane):
    core = lax.axis_index("lx") % 2
    at = 7 - lax.axis_index("af") * 7
    column = jnp.where(lax.axis_index("ly") % 2 == core, 15, 0)

    def picker(rows, tiles):
        row = lax.broadcasted_iota(jnp.int32, (rows, 16 * tiles), 0)
        cell = lax.broadcasted_iota(jnp.int32, (rows, 16 * tiles), 1)
        return jnp.where(cell == row * 16 + column, 1.0, 0.0).astype(BF)

    pick = picker(8, 8)

    def ends(tile, to):
        got = jnp.dot(pick, tile.reshape(128, C), preferred_element_type=F32)
        line[pl.ds(to, 1)] = got.astype(BF)[None]

    for src, to in ((g, core * 8 + 1), (other, 9 - core * 8)):
        for n in range(8):
            ends(src[:, n], to + n)
        plane[pl.ds(to, 8)] = src[pl.ds(at, 1)].reshape(8, 16, C)
    z = lax.axis_index("lx") // 2
    for n, src in enumerate((alpha, beta)):
        to = 17 * (core ^ n)
        inside = jnp.where(to == 0, z > 0, z < 3)
        outer[n] = jnp.where(inside, src[...].astype(F32), 0.0).astype(BF)
        ends(outer[n], to)
        plane[pl.ds(to, 1)] = outer[n, pl.ds(at, 1)]
    half[...] = plane[pl.ds(9 * core, 9)]
    got = jnp.dot(picker(24, 18), plane[...].reshape(288, C), preferred_element_type=F32)
    corner[...] = got[:18].astype(BF)


def edges(g, other, alpha, beta):
    return pl.pallas_call(
        edges_kernel,
        out_shape=(
            sds((18, 8, C), BF),
            sds((9, 16, C), BF),
            sds((18, C), BF),
            sds((2, 8, 16, C), BF),
        ),
        scratch_shapes=[pltpu.VMEM((18, 16, C), BF)],
        compiler_params=params(10),
        cost_estimate=BRIEF,
        name="edges",
    )(g, other, alpha, beta)


def turn_kernel(own, other, out, both):
    core = lax.axis_index("lx") % 2
    mine = lax.axis_index("lx") * 8 + lax.axis_index("ly")
    both[:, pl.ds(core * 8, 8)] = own[...]
    both[:, pl.ds(8 - core * 8, 8)] = other[...]
    cells = both[...].reshape(2048, C)
    row = lax.broadcasted_iota(jnp.int32, (C, C), 0)
    fives, tens, twenties, eighties = row * 13108 >> 16, row * 6554 >> 16, row * 52429 >> 20, row * 52429 >> 22
    first, second = eighties, twenties & 3
    first, second = first ^ (first >> 1), second ^ (second >> 1)
    z, x = jnp.where(core == 0, first, second), jnp.where(core == 0, second, first)
    chunk = mine ^ (z * 16 + (tens & 1) * 8 + (fives & 1) * 4 + x)
    lane = lax.broadcasted_iota(jnp.int32, (C, C), 1)
    pick = jnp.where(lane == chunk * 5 + row - fives * 5, 1.0, 0.0).astype(BF)
    out[...] = lax.dot_general(
        pick, cells, (((1,), (1,)), ((), ())), preferred_element_type=F32
    ).astype(BF)


def turn(own, other):
    return pl.pallas_call(
        turn_kernel,
        out_shape=sds((C, 2048), BF),
        scratch_shapes=[pltpu.VMEM((8, 16, 16, C), BF)],
        compiler_params=params(12),
        cost_estimate=LONG,
        name="turn",
    )(own, other)


def spread(tile, left, right):
    n = tile.shape[0]
    rows = n * 16
    flat = tile.astype(F32).reshape(rows, C)
    col = lax.broadcasted_iota(jnp.int32, (n, 16, C), 1).reshape(rows, C)
    ends = jnp.broadcast_to(right.reshape(n, 1, C), (n, 16, C)).reshape(rows, C)
    heads = jnp.broadcast_to(left.reshape(n, 1, C), (n, 16, C)).reshape(rows, C)
    up = jnp.where(col == 15, ends, pltpu.roll(flat, rows - 1, 0)).astype(BF)
    down = jnp.where(col == 0, heads, pltpu.roll(flat, 1, 0)).astype(BF)
    shifts = (up, tile.reshape(rows, C), down)
    pad = jnp.zeros((rows, HALF - 480), BF)
    lanes = [v[:, :160] for v in shifts] + [pad] + [v[:, 160:] for v in shifts] + [pad]
    return jnp.concatenate(lanes, axis=1).reshape(n, 16, LANES)


def tiles_kernel(
    g, other, outer, line, line_other, half, half_other, corner, corner_other, turned,
    shifted, keep, one, three, far, plane,
):
    core = lax.axis_index("lx") % 2
    af = lax.axis_index("af")
    ly = lax.axis_index("ly")
    side = ly % 2

    def order(mine, theirs):
        mine, theirs = mine.astype(F32), theirs.astype(F32)
        left = jnp.where(side == core, theirs, mine)
        right = jnp.where(side == core, mine, theirs)
        return jnp.where(ly > 0, left, 0.0), jnp.where(ly < 7, right, 0.0)

    def put(tile, at):
        lines = order(line[pl.ds(at, 1)][0], line_other[pl.ds(at, 1)][0])
        shifted[1:9, pl.ds(at, 1)] = spread(tile, *lines)[:, None]

    for src, at in ((g, core * 8 + 1), (other, 9 - core * 8)):

        def row(n, carry, src=src, at=at):
            put(src[:, pl.ds(n, 1)].reshape(8, 16, C), at + n)
            return carry

        lax.fori_loop(0, 8, row, 0, unroll=8)
    put(outer[0], core * 17)
    put(outer[1], 17 - core * 17)
    plane[pl.ds(9 * core, 9)] = half[...]
    plane[pl.ds(9 - 9 * core, 9)] = half_other[...]
    lines = order(corner[...], corner_other[...])
    shifted[pl.ds(9 - af * 9, 1)] = spread(plane[...], *lines)[None]
    shifted[pl.ds(af * 9, 1)] = jnp.zeros((1, 18, 16, LANES), BF)
    lanes = pl.ds(pl.multiple_of(core * HALF, HALF), HALF)
    for pq in range(9):
        p, q = pq // 3, pq % 3
        cells = shifted[2 - p : 10 - p, 2 - q : 18 - q, :, lanes].reshape(2048, HALF)
        tile = jnp.dot(turned[...], cells, preferred_element_type=F32)
        keep[pq] = tile[0:80]
        for n, ref in enumerate((one, three, far)):
            ref[pq] = tile[80 * n + 80 : 80 * n + 160].astype(BF)


def tiles(*operands):
    piece = sds((9, 80, HALF), BF)
    return pl.pallas_call(
        tiles_kernel,
        out_shape=(sds((10, 18, 16, LANES), BF), sds((9, 80, HALF), F32), piece, piece, piece),
        scratch_shapes=[pltpu.VMEM((18, 16, C), BF)],
        compiler_params=params(28),
        cost_estimate=LONG,
        name="tiles",
    )(*operands)


def flipped(weight, pq, start, rows):
    row = lax.broadcasted_iota(jnp.int32, (rows, C), 0)
    lane = lax.broadcasted_iota(jnp.int32, (rows, C), 1)
    pick = jnp.where(lane == row + start, 1.0, 0.0).astype(BF)
    taps = weight[3 * pq : 3 * pq + 3].reshape(480, C)
    turned = lax.dot_general(pick, taps, (((1,), (1,)), ((), ())), preferred_element_type=F32)
    return jnp.concatenate([turned.astype(BF), jnp.zeros((rows, HALF - 480), BF)], axis=1)


def flip_kernel(weight, after, out):
    core = lax.axis_index("lx") % 2
    for pq in range(9):
        out[pq] = flipped(weight, pq, core * 160, 160)


def flip(weight, after):
    vmem, hbm = pl.BlockSpec(memory_space=pltpu.VMEM), pl.BlockSpec(memory_space=pl.ANY)
    return pl.pallas_call(
        flip_kernel,
        out_shape=sds((9, 160, HALF), BF),
        in_specs=[vmem, hbm],
        out_specs=vmem,
        compiler_params=params(20),
        cost_estimate=BRIEF,
        name="flip",
    )(weight, after)


def half_sum(shifted, taps, first, emit):
    core = lax.axis_index("lx") % 2
    lanes = pl.ds(pl.multiple_of(first * HALF, HALF), HALF)
    for p in range(3):
        value = None
        for q in range(3):
            rows = pl.ds(core * 8 + 2 - q, 8)
            cells = shifted[2 - p : 10 - p, rows, :, lanes].reshape(1024, HALF)
            term = lax.dot_general(
                taps(3 * p + q), cells, (((1,), (1,)), ((), ())), preferred_element_type=F32
            )
            value = term if value is None else value + term
        emit(p, value)


def own_kernel(shifted, own, out):
    def emit(p, value):
        out[...] = value if p == 0 else out[...] + value

    half_sum(shifted, lambda pq: flipped(own, pq, 0, C), lax.axis_index("af"), emit)


def own_half(shifted, own):
    return pl.pallas_call(
        own_kernel,
        out_shape=sds((C, 1024), F32),
        compiler_params=params(20),
        cost_estimate=BRIEF,
        name="own_half",
    )(shifted, own)


def other_kernel(shifted, far, near_low, near_high, partial, out, total):
    core = lax.axis_index("lx") % 2
    pad = jnp.zeros((160, HALF - 480), F32)

    def taps(pq):
        own = far[pq].astype(F32)
        near = jnp.concatenate([near_low[pq], near_high[pq]], axis=0).astype(F32)
        near = jnp.concatenate([near, pad], axis=1)
        low, high = jnp.where(core == 0, own, near), jnp.where(core == 0, near, own)
        return jnp.concatenate([low, high], axis=0).astype(BF)

    def emit(p, value):
        value = value + (partial if p == 0 else total)[...]
        if p < 2:
            total[...] = value
        else:
            out[...] = value.T.astype(BF).reshape(8, 8, 16, C)

    half_sum(shifted, taps, 1 - lax.axis_index("af"), emit)


def other_half(shifted, far, near, partial):
    return pl.pallas_call(
        other_kernel,
        out_shape=sds((8, 8, 16, C), BF),
        scratch_shapes=[pltpu.VMEM((C, 1024), F32)],
        compiler_params=params(24),
        cost_estimate=BRIEF,
        name="other_half",
    )(shifted, far, *near, partial)


def fold_kernel(keep, one, three, far, *outs):
    parts = [[], [], [], []]
    for pq in range(9):
        total = keep[pq]
        for ref in (one, three, far):
            total = total + ref[pq].astype(F32)
        for n in range(4):
            parts[n].append(total[20 * n : 20 * n + 20])
    for part, ref in zip(parts, outs):
        ref[...] = jnp.concatenate(part, axis=0).astype(ref.dtype)


def fold(*operands):
    piece = sds((180, HALF), BF)
    return pl.pallas_call(
        fold_kernel,
        out_shape=(sds((180, HALF), F32), piece, piece, piece),
        compiler_params=params(12),
        cost_estimate=BRIEF,
        name="fold",
    )(*operands)


def cut_kernel(keep, r1, r2, r3, mine, s1, s2, s3, s4):
    home = lax.axis_index("af") == lax.axis_index("lx") % 2
    total = keep[...]
    for ref in (r1, r2, r3):
        total = total + ref[...].astype(F32)
    same, far_same, other, far_other = (
        jnp.concatenate([total[20 * n + at : 20 * n + at + 5] for n in range(9)], axis=0)
        for at in (0, 5, 10, 15)
    )
    mine[...] = same
    s1[...] = jnp.where(home, other, same).astype(BF)
    s2[...] = jnp.where(home, far_other, far_same).astype(BF)
    s3[...] = jnp.where(home, far_same, other).astype(BF)
    s4[...] = far_other.astype(BF)


def cut(*operands):
    return pl.pallas_call(
        cut_kernel,
        out_shape=(sds((45, HALF), F32),) + (sds((45, HALF), BF),) * 4,
        compiler_params=params(),
        cost_estimate=BRIEF,
        name="cut",
    )(*operands)


def last_kernel(scale, mine, r1, r2, r3, r4, out):
    home = lax.axis_index("af") == lax.axis_index("lx") % 2
    total = r1[...].astype(F32) + r2[...].astype(F32) + r3[...].astype(F32)
    total = (total + jnp.where(home, mine[...], r4[...].astype(F32))) * scale
    for pq in range(9):
        for r in range(3):
            out[:, 3 * pq + r, :] = total[5 * pq : 5 * pq + 5, 160 * r : 160 * r + 160]


def last(scale, *operands):
    return pl.pallas_call(
        functools.partial(last_kernel, scale),
        out_shape=sds((5, 27, 160), F32),
        compiler_params=params(),
        cost_estimate=BRIEF,
        name="last",
    )(*operands)


def body(grad_out, inputs, weight):
    core = lax.axis_index("lx") % 2
    scale = 1.0 / math.sqrt(16 * 64 * 128)

    grad_other = swap_core(grad_out)
    inputs_other = swap_core(inputs)
    outer = lax.dynamic_slice_in_dim(grad_out, core * 7, 1, 1).reshape(8, 16, C)
    alpha = send(outer, lambda a, b, c: ((a + 2 * (a % 2) - 1) % 8, b, c))
    beta = send(outer, lambda a, b, c: ((a + 4 * (a % 2) - 2) % 8, b, c))
    turned = turn(inputs, inputs_other)
    alpha, beta, grad_other, turned = lax.optimization_barrier((alpha, beta, grad_other, turned))

    line, plane, corner, outer = edges(grad_out, grad_other, alpha, beta)
    quarter = flip(weight, corner)

    def side(a, b):
        return b ^ 1 if a % 2 == 0 else (b + 2 * (b % 2) - 1) % 8

    plane = send(plane, lambda a, b, c: (a, b, c ^ 1))
    line = send(line, lambda a, b, c: (a, side(a, b), c))
    corner = send(corner, lambda a, b, c: (a, side(a, b), c ^ 1))
    plane, line, corner, quarter = lax.optimization_barrier((plane, line, corner, quarter))
    line_other, corner_other, plane_other = swap_core(line), swap_core(corner), swap_core(plane)

    far = send(quarter, lambda a, b, c: (a, b ^ (4 * (a % 2)), c ^ 1))

    shifted, keep, one, three, opposite = tiles(
        grad_out, grad_other, outer,
        line, line_other, plane, plane_other, corner, corner_other, turned,
    )

    def ring(s, second):
        return lambda a, b, c: (a ^ (2 * s), b, c) if a % 2 == second else (a, b ^ s, c)

    opposite, one, three = send(opposite, ring(2, 0)), send(one, ring(1, 0)), send(three, ring(3, 0))
    grad_input = own_half(shifted, weight)
    grad_input, far = lax.optimization_barrier((grad_input, far))
    near = [swap_core(far[:, n : n + 80, :480]) for n in (0, 80)]
    grad_input = other_half(shifted, far, near, grad_input)
    grad_input, opposite, one, three = lax.optimization_barrier((grad_input, opposite, one, three))

    keep, one, three, far = fold(keep, one, three, opposite)
    far, one, three = send(far, ring(2, 1)), send(one, ring(1, 1)), send(three, ring(3, 1))
    mine, *sums = cut(keep, far, one, three)

    def either(home, away):
        return lambda a, b, c: home(a, b, c) if a % 2 == c else away(a, b, c)

    steps = (
        either(lambda a, b, c: (a ^ 1, b, c), lambda a, b, c: (a, b, c ^ 1)),
        either(lambda a, b, c: (a ^ 1, b ^ 4, c), lambda a, b, c: (a, b ^ 4, c ^ 1)),
        either(lambda a, b, c: (a, b ^ 4, c), lambda a, b, c: (a ^ 1, b, c ^ 1)),
        either(lambda a, b, c: (a, b, c), lambda a, b, c: (a ^ 1, b ^ 4, c ^ 1)),
    )
    sums = [send(sums[n], steps[n]) for n in (2, 1, 0, 3)]
    grad_weight = last(scale, mine, *sums)
    return (grad_input, jnp.transpose(grad_weight, (1, 2, 0)))


def solution(mesh):
    placed = (P("af", "lx", "ly", None), P("af", "lx", "ly", None), P(None, "af", None))
    return jax.shard_map(
        body,
        mesh=mesh,
        in_specs=placed,
        out_specs=(P("af", "lx", "ly", None), P(None, "af", ("lx", "ly"))),
        check_vma=False,
    )
```
